128 devices in a mesh: band: 32 (over x, y, core), patch: 4 (over z).
Axes of the slice: x: 4, y: 4, z: 4, core: 2. Of those that a mesh axis runs over, the one named last changes fastest.
Arguments:
- grid_feat: bfloat16 [262144, 227], P(('band', 'patch')), may hold values from -6 to 6
- w_embed: bfloat16 [227, 512], replicated, may hold values from -0.375 to 0.375
- w_send: bfloat16 [512, 512], replicated, may hold values from -0.25 to 0.25
- edge_vec: bfloat16 [512], replicated, may hold values from -5 to 5
- g2m_sender: int32 [128, 4096], P(('band', 'patch')), may hold values from 0 to 2047
- g2m_weight: float32 [128, 4096], P(('band', 'patch')), may hold values from 0.25 to 4
- g2m_target: int32 [128, 4096], P(('band', 'patch')), may hold values from -1 to 1023, as said below
- w_agg: bfloat16 [512, 512], replicated, may hold values from -0.25 to 0.25
- halo_rows: int32 [128, 4, 128], P(('band', 'patch')), may hold values from 0 to 1023
- mesh_src: int32 [131072, 6], P(('band', 'patch')), may hold values from 0 to 1535
- w_src: bfloat16 [2, 512, 512], replicated, may hold values from -0.25 to 0.25
- w_dst: bfloat16 [2, 512, 512], replicated, may hold values from -0.25 to 0.25
- w_up: bfloat16 [2, 1024, 512], replicated, may hold values from -0.1875 to 0.1875
- w_down: bfloat16 [2, 512, 512], replicated, may hold values from -0.25 to 0.25
- ln_gain: float32 [2, 512], replicated, may hold values from 0.1 to 1.9
Outputs:
- mesh_out: bfloat16 [131072, 512], P(('band', 'patch'))
The draws below stay inside these ranges and needn't reach their ends.
Inputs may be any that keep to these rules, and one draw needn't show every extreme that they name: `g2m_target`: -1 marks an empty slot; other values are mesh rows of the receiving block. `halo_rows`: rows of the sending block. `mesh_src`: rows of the receiving block's extended table.
All inputs are finite; a program needn't handle non-finite values.
Results may differ from the reference program's by a relative error of at most 0.009.
Values may be sent and summed in bfloat16 or wider, within the bound.
A program may use at most 64 MiB of HBM per device.

```python
import math
from functools import partial
import jax
import jax.numpy as jnp
from jax import lax

LATENT = 512
VARS = 227
GRID_DEV = 2048
MESH_DEV = 1024
EDGE_DEV = 4096
HALO = 128
DEG = 6
LAYERS = 2
OWNERS = 128
GRID = 262144
MESH = 131072
N_BAND = 32
N_PATCH = 4


def draw_g2m_target(key, part):
    key = jax.random.fold_in(key, 11)
    first_key, second_key = jax.random.split(key, 2)
    slot_count = EDGE_DEV // OWNERS
    row_ids = jax.random.randint(first_key, (OWNERS, OWNERS, slot_count), 0, MESH_DEV)
    row_ids = row_ids.at[0, 0, 0].set(MESH_DEV - 1)
    live_count = jax.random.randint(second_key, (OWNERS, OWNERS, 1), slot_count // 3, slot_count + 1)
    live_count = live_count.at[0, 0, 0].set(slot_count)
    live_count = live_count.at[0, 1, 0].set(slot_count // 3)
    slot_pos = jnp.arange(slot_count, dtype=jnp.int32)[None, None, :]
    result = jnp.where(slot_pos < live_count, row_ids, -1)
    return result.reshape(OWNERS, EDGE_DEV).astype(jnp.int32)


def place_ends(values, own_key, smallest, largest):
    longest = values.shape.index(max(values.shape))
    spots = []
    for shift in (0, 1):
        where = [jax.random.randint(jax.random.fold_in(own_key, axis), (), 0, length) for axis, length in enumerate(values.shape)]
        where[longest] = (where[longest] + shift) % values.shape[longest]
        spots.append(tuple(where))
    return values.at[spots[0]].set(smallest).at[spots[1]].set(largest)


def steps_of(own_key, dims, shards, smallest, high):
    def one(axis_at, parts):
        draws = jax.random.uniform(jax.random.fold_in(jax.random.fold_in(own_key, 6), axis_at), (parts,), jnp.float32, smallest / len(shards), high / len(shards))
        return jnp.repeat(jnp.exp(draws), dims[axis_at] // parts).reshape((-1,) + (1,) * (len(dims) - axis_at - 1))

    level = one(*shards[0])
    for cut in shards[1:]:
        level = level * one(*cut)
    return level


def scatter_about(key, shape, width, bound, cuts=(), held_as=jnp.bfloat16):
    drawn = jax.random.normal(key, shape, jnp.float32) * width
    if len(cuts) > 0:
        drawn = steps_of(key, shape, cuts, -0.22, 0.18) * drawn
    return jnp.clip(drawn, min=-bound, max=bound).astype(held_as)


def setup_inputs(seed: int = 0) -> dict:
    keys = jax.random.split(jax.random.key(seed), 16)
    grid_feat = scatter_about(keys[0], (GRID, VARS), 1.0, 6.0, ((0, 128),))
    w_embed = scatter_about(keys[1], (VARS, LATENT), VARS ** -0.5, 0.375)
    w_send = scatter_about(keys[2], (LATENT, LATENT), LATENT ** -0.5, 0.25)
    edge_vec = scatter_about(keys[3], (LATENT,), 1.0, 5.0)
    g2m_sender = place_ends(jax.random.randint(keys[4], (OWNERS, EDGE_DEV), 0, GRID_DEV), jax.random.fold_in(keys[4], 1), 0, GRID_DEV - 1).astype(jnp.int32)
    g2m_weight = jnp.clip(jnp.exp(math.log(4.0) - 2.7725887 * jax.random.uniform(keys[5], (OWNERS, EDGE_DEV), jnp.float32) ** steps_of(keys[5], (OWNERS, EDGE_DEV), ((0, 128),), -0.2, 0.2)), 0.25, 4.0)
    g2m_target = draw_g2m_target(jax.random.fold_in(keys[15], 71), 0)
    w_agg = scatter_about(keys[7], (LATENT, LATENT), LATENT ** -0.5, 0.25)
    halo_rows = place_ends(jax.random.randint(keys[8], (OWNERS, 4, HALO), 0, MESH_DEV), jax.random.fold_in(keys[8], 1), 0, MESH_DEV - 1).astype(jnp.int32)
    mesh_src = place_ends(jax.random.randint(keys[9], (MESH, DEG), 0, MESH_DEV + 4 * HALO), jax.random.fold_in(keys[9], 1), 0, (MESH_DEV + 4 * HALO) - 1).astype(jnp.int32)
    w_src = scatter_about(keys[10], (LAYERS, LATENT, LATENT), LATENT ** -0.5, 0.25)
    w_dst = scatter_about(keys[11], (LAYERS, LATENT, LATENT), LATENT ** -0.5, 0.25)
    w_up = scatter_about(keys[12], (LAYERS, 2 * LATENT, LATENT), (2 * LATENT) ** -0.5, 0.1875)
    w_down = scatter_about(keys[13], (LAYERS, LATENT, LATENT), LATENT ** -0.5, 0.25)
    ln_gain = jnp.clip(1.0 + 0.18 * jax.random.normal(keys[14], (LAYERS, LATENT), jnp.float32), 0.1, 1.9)
    return dict(grid_feat=grid_feat, w_embed=w_embed, w_send=w_send, edge_vec=edge_vec, g2m_sender=g2m_sender, g2m_weight=g2m_weight, g2m_target=g2m_target, w_agg=w_agg, halo_rows=halo_rows, mesh_src=mesh_src, w_src=w_src, w_dst=w_dst, w_up=w_up, w_down=w_down, ln_gain=ln_gain)


def node_update(w_src_l, w_dst_l, w_up_l, w_down_l, gain_l, packed):
    extended, own_rows, sources = packed
    latent_width = own_rows.shape[1]
    from_send = jnp.dot(extended, w_src_l, preferred_element_type=jnp.float32)
    at_recv = jnp.dot(own_rows, w_dst_l, preferred_element_type=jnp.float32)
    edge_terms = jax.nn.silu(jnp.take(from_send, sources, axis=0) + at_recv[:, None, :])
    edge_sum = lax.optimization_barrier(jnp.sum(edge_terms, axis=1)).astype(jnp.bfloat16)
    hidden = jax.nn.silu(jnp.dot(own_rows, w_up_l[:latent_width], preferred_element_type=jnp.float32) + jnp.dot(edge_sum, w_up_l[latent_width:], preferred_element_type=jnp.float32)).astype(jnp.bfloat16)
    mixed = jnp.dot(hidden, w_down_l, preferred_element_type=jnp.float32)
    centre = mixed - lax.optimization_barrier(jnp.mean(mixed, axis=1, keepdims=True))
    spread = lax.optimization_barrier(jnp.mean(centre * centre, axis=1, keepdims=True))
    normed = centre * lax.rsqrt(spread + 1e-05) * gain_l.astype(jnp.float32)[None, :]
    return (own_rows.astype(jnp.float32) + normed).astype(jnp.bfloat16)

def reference(grid_feat, w_embed, w_send, edge_vec, g2m_sender, g2m_weight, g2m_target, w_agg, halo_rows, mesh_src, w_src, w_dst, w_up, w_down, ln_gain):
    owners = N_BAND * N_PATCH
    latent_width = w_embed.shape[1]
    grid_lat = jax.nn.silu(jnp.dot(grid_feat, w_embed, preferred_element_type=jnp.float32)).astype(jnp.bfloat16)
    projected = jnp.dot(grid_lat, w_send, preferred_element_type=jnp.float32).reshape(owners, GRID_DEV, latent_width)

    def make_messages(packed):
        block_proj, senders, lengths = packed
        pre_act = jnp.take(block_proj, senders, axis=0) + lengths[:, None].astype(jnp.float32) * edge_vec.astype(jnp.float32)[None, :]
        return jax.nn.silu(pre_act).astype(jnp.bfloat16)
    messages = lax.map(make_messages, (projected, g2m_sender, g2m_weight))
    slot_count = EDGE_DEV // owners
    routed = messages.reshape(owners, owners, slot_count, latent_width).transpose(1, 0, 2, 3).reshape(owners, EDGE_DEV, latent_width)

    def block_sum(packed):
        arrived, targets = packed
        segment_ids = jnp.where(targets < 0, MESH_DEV, targets).astype(jnp.int32)
        totals = jax.ops.segment_sum(arrived.astype(jnp.float32), segment_ids, num_segments=MESH_DEV + 1)
        return totals[:MESH_DEV].astype(jnp.bfloat16)
    summed = lax.map(block_sum, (routed, g2m_target)).reshape(owners * MESH_DEV, latent_width)
    mesh_h = jax.nn.silu(jnp.dot(summed, w_agg, preferred_element_type=jnp.float32)).astype(jnp.bfloat16)
    mesh_h = mesh_h.reshape(N_BAND, N_PATCH, MESH_DEV, latent_width)
    sources = mesh_src.reshape(owners, MESH_DEV, DEG)
    for section_index in range(LAYERS):
        flat_rows = mesh_h.reshape(owners, MESH_DEV, latent_width)
        picked = jax.vmap(lambda block_rows, chosen: jnp.take(block_rows, chosen.reshape(-1), axis=0))(flat_rows, halo_rows)
        picked = picked.reshape(N_BAND, N_PATCH, 4, HALO, latent_width)
        from_low = jnp.roll(picked[:, :, 0], 1, axis=1)
        from_high = jnp.roll(picked[:, :, 1], -1, axis=1)
        zero_band = jnp.zeros((1, N_PATCH, HALO, latent_width), jnp.bfloat16)
        from_south = jnp.concatenate([zero_band, picked[:-1, :, 2]], axis=0)
        from_north = jnp.concatenate([picked[1:, :, 3], zero_band], axis=0)
        extended = jnp.concatenate([mesh_h, from_low, from_high, from_south, from_north], axis=2)
        extended = extended.reshape(owners, MESH_DEV + 4 * HALO, latent_width)
        update = partial(node_update, w_src[section_index], w_dst[section_index], w_up[section_index], w_down[section_index], ln_gain[section_index])
        mesh_h = lax.map(update, (extended, flat_rows, sources)).reshape(N_BAND, N_PATCH, MESH_DEV, latent_width)
    return mesh_h.reshape(owners * MESH_DEV, latent_width)
```

```python
import jax
import jax.numpy as jnp
from jax import lax
from jax.experimental import pallas as pl
from jax.experimental.pallas import tpu as pltpu
from jax.sharding import PartitionSpec as P

MESH = pl.DeviceIdType.MESH
BF16 = jnp.bfloat16
F32 = jnp.float32
VARS, D, W = 227, 512, 256
GRID, M, SLOTS, OWNERS = 2048, 1024, 32, 128
HALO, DEG, LAYERS = 128, 6, 2
TILE = 128
CHUNK = 256
PAIRS = 16


def dot(a, b):
    return jnp.dot(a, b, preferred_element_type=F32)


def half_silu(h):
    return h + h * jnp.tanh(h)


def column(row):
    return jnp.transpose(jnp.broadcast_to(row, (TILE, TILE)))


def lanes(shape):
    return lax.broadcasted_iota(jnp.int32, shape, len(shape) - 1)


def put_rows(ref, at, value):
    rows = value.shape[0]
    for j in range(D // TILE):
        ref[pl.ds(at + j, rows, stride=4), :] = value[:, j * TILE : (j + 1) * TILE]


def kernel(
    feat_hbm, embed_hbm, send_hbm, vec_hbm, sender_hbm, length_hbm, target_hbm, agg_hbm, halo_hbm, src_hbm,
    wsrc_hbm, wdst_hbm, wup_hbm, wdown_hbm, gain_hbm,
    out_hbm,
    feat, embed, wsend, vec, sender, length, target, wagg, halo_ids, src, wsrc, wdst, wup, wdown, gain,
    feat_pad, wcat, pick, outbox, inbox, scatter, msgs, summed, ext, halo_pick, halo_out, halo_in,
    table, recv, sums, esum, up, src_v, src_s,
    in_sem, idx_sem, send_sem, recv_sem, halo_send, halo_recv, out_sem, ready,
):
    band, z = lax.axis_index("band"), lax.axis_index("patch")
    x, y, core = band // 8, (band // 2) % 4, band % 2
    me = band * 4 + z

    def loads():
        pairs = (
            (feat_hbm, feat), (sender_hbm, sender), (length_hbm, length), (embed_hbm, embed), (vec_hbm, vec),
            (target_hbm, target), (src_hbm, src), (halo_hbm, halo_ids), (send_hbm, wsend), (agg_hbm, wagg),
            (wsrc_hbm, wsrc), (wdst_hbm, wdst), (wup_hbm, wup), (wdown_hbm, wdown), (gain_hbm, gain),
        )
        return [pltpu.make_async_copy(a, b, in_sem.at[i]) for i, (a, b) in enumerate(pairs)]

    copies = loads()
    for copy in copies:
        copy.start()

    plane = [((((x + i) % 4) * 4 + (y + j) % 4) * 2 + core, z) for i in range(4) for j in range(4) if i or j]
    line = [(band // 2 * 2 + (core + i) % 2, (z + j) % 4) for i in range(2) for j in range(4) if i or j]
    barrier = pltpu.get_barrier_semaphore()
    for device in plane + line:
        pl.semaphore_signal(barrier, inc=1, device_id=device, device_id_type=MESH)

    feat_pad[W - 32 : W, :] = jnp.zeros((32, GRID), BF16)
    for i in (0, 1, 2):
        copies[i].wait()
    feat_pad[0:VARS, :] = feat[...]

    def pick_window(w):
        def band_of(i, j):
            return ((x + i) % 4 * 4 + (y + i + w) % 4) * 2 + (core + j) % 2

        for i in range(4):
            for j in range(2):
                ids = column(sender[pl.ds(band_of(i, j), 1), :])
                rows = slice((i * 2 + j) * TILE, (i * 2 + j + 1) * TILE)
                for k in range(GRID // TILE):
                    hit = ids == lanes((TILE, TILE)) + k * TILE
                    pick[rows, k * TILE : (k + 1) * TILE] = hit.astype(F32).astype(BF16)

    def rows_window(w):
        for i in range(4):
            both = lax.dot_general(
                pick[i * 2 * TILE : (i + 1) * 2 * TILE, :], feat_pad[...], (((1,), (1,)), ((), ())),
                preferred_element_type=F32,
            )
            for j in range(2):
                to = ((x + i) % 4 * 4 + (y + i + w) % 4) * 2 + (core + j) % 2
                rows = both[j * TILE : (j + 1) * TILE, :]
                long = column(length[pl.ds(to, 1), :])
                first = long.astype(BF16).astype(F32)
                second = (long - first).astype(BF16).astype(F32)
                third = long - first - second
                lane = lanes((TILE, TILE)) + TILE
                tail = rows[:, TILE:]
                tail = jnp.where(lane == VARS, first, tail)
                tail = jnp.where(lane == VARS + 1, second, tail)
                tail = jnp.where(lane == VARS + 2, third, tail)
                outbox[to, :, 0:TILE] = rows[:, :TILE].astype(BF16)
                outbox[to, :, TILE:W] = tail.astype(BF16)

    def send_window(w):
        for dz in range(4):
            for i in range(4):
                for j in range(2):
                    to = ((x + i) % 4 * 4 + (y + i + w) % 4) * 2 + (core + j) % 2
                    to_z = (z + dz) % 4
                    part = outbox.at[to, pl.ds(pl.multiple_of(to_z * SLOTS, SLOTS), SLOTS)]

                    def remote():
                        pltpu.make_async_remote_copy(
                            src_ref=part, dst_ref=inbox.at[me], send_sem=send_sem.at[0],
                            recv_sem=recv_sem.at[band // 2], device_id=(to, to_z), device_id_type=MESH,
                        ).start()

                    if i == 0 and j == 0 and dz == 0:
                        pl.when(w != 0)(remote)

                        @pl.when(w == 0)
                        def _():
                            pltpu.make_async_copy(part, inbox.at[me], recv_sem.at[band // 2]).start()
                    else:
                        remote()

    pick_window(0)
    pl.semaphore_wait(barrier, len(plane) + len(line))
    for device in line:
        pl.semaphore_signal(ready, inc=1, device_id=device, device_id_type=MESH)
    rows_window(0)
    pl.semaphore_wait(ready, len(line))
    send_window(0)

    @pl.loop(1, 4)
    def _(w):
        pick_window(w)
        rows_window(w)
        send_window(w)

    for copy in copies[3:]:
        copy.wait()
    wcat[...] = jnp.zeros((W, 2 * D), BF16)
    wcat[0:VARS, 0:D] = (embed[...].astype(F32) * 0.5).astype(BF16)
    edge_row = jnp.broadcast_to((vec[...].astype(F32) * 0.5).astype(BF16), (3, D))
    wcat[VARS : VARS + 3, D : 2 * D] = edge_row
    parity = (lanes((1, TILE)) + 1) % 2 * 4 + 4
    for k in range(DEG):
        for j in range(M // TILE):
            ids = src[k : k + 1, j * TILE : (j + 1) * TILE] * 4 + parity
            src_v[pl.ds(k * M + j * TILE, TILE)] = ids.reshape(TILE)
    src_copy = pltpu.make_async_copy(src_v, src_s, idx_sem)
    src_copy.start()
    for i in range(4):
        ids = column(halo_ids[i : i + 1, :])
        for k in range(M // TILE):
            hit = ids == lanes((TILE, TILE)) + k * TILE
            halo_pick[i * TILE : (i + 1) * TILE, k * TILE : (k + 1) * TILE] = hit.astype(F32).astype(BF16)
    summed[...] = jnp.zeros((M, D), F32)
    ends = (M + 4 * HALO) * 4 + 8
    table[0:8, :] = jnp.zeros((8, TILE), F32)
    table[ends : ends + 8, :] = jnp.zeros((8, TILE), F32)

    @pl.loop(0, 4)
    def _(w):
        def group(i):
            return (x + 4 - i) % 4 * 4 + (y + 8 - i - w) % 4

        for i in range(4):
            for h in range(2):
                ids = jnp.broadcast_to(target[pl.ds(group(i) * 2 + h, 1), :], (TILE, TILE))
                for k in range(M // TILE):
                    hit = ids == lax.broadcasted_iota(jnp.int32, (TILE, TILE), 0) + k * TILE
                    scatter[k * TILE : (k + 1) * TILE, (i * 2 + h) * TILE : (i * 2 + h + 1) * TILE] = hit.astype(
                        F32
                    ).astype(BF16)
        for i in range(4):
            g = group(i)
            part = inbox.at[pl.ds(pl.multiple_of(g * 8, 8), 8)]
            pltpu.make_async_copy(part, part, recv_sem.at[g]).wait()
            rows = inbox[pl.ds(pl.multiple_of(g * 8, 8), 8)].reshape(CHUNK, W)
            first = dot(rows, wcat[...])
            latent = half_silu(first[:, :D]).astype(BF16)
            pre = dot(latent, wsend[...]) * 0.5 + first[:, D:]
            msgs[i * CHUNK : (i + 1) * CHUNK, :] = half_silu(pre).astype(BF16)
        for k in range(M // CHUNK):
            rows = slice(k * CHUNK, (k + 1) * CHUNK)
            summed[rows, :] += dot(scatter[rows, :], msgs[...])

    for k in range(M // CHUNK):
        rows = slice(k * CHUNK, (k + 1) * CHUNK)
        ext[rows, :] = half_silu(dot(summed[rows, :].astype(BF16), wagg[...]) * 0.5).astype(BF16)
    src_copy.wait()

    neighbours = ((band, (z + 1) % 4), (band, (z + 3) % 4), ((band + 1) % 32, z), ((band + 31) % 32, z))
    low = lax.broadcasted_iota(jnp.int32, (8, TILE), 0) < 4

    @pl.loop(0, LAYERS)
    def _(layer):
        halos = []
        for i in range(4):
            rows = slice(i * HALO, (i + 1) * HALO)
            halo_out[layer, rows, :] = dot(halo_pick[rows, :], ext[...]).astype(BF16)
            copy = pltpu.make_async_remote_copy(
                src_ref=halo_out.at[layer, rows], dst_ref=halo_in.at[layer, rows],
                send_sem=halo_send.at[layer, i], recv_sem=halo_recv.at[layer, i],
                device_id=neighbours[i], device_id_type=MESH,
            )
            copy.start()
            halos.append(copy)
        for k in range(M // CHUNK):
            rows = slice(k * CHUNK, (k + 1) * CHUNK)
            own = ext[rows, :]
            put_rows(table, 8 + k * CHUNK * 4, dot(own, wsrc[layer]) * 0.5)
            put_rows(recv, k * CHUNK * 4, dot(own, wdst[layer]) * 0.5)
            up[rows, :] = dot(own, wup[layer, 0:D, :])
        for i in range(4):
            halos[i].wait()
            rows = slice(i * HALO, (i + 1) * HALO)
            value = dot(halo_in[layer, rows, :], wsrc[layer]) * 0.5
            if i == 2:
                value = jnp.where(band == 0, 0.0, value)
            if i == 3:
                value = jnp.where(band == 31, 0.0, value)
            put_rows(table, 8 + (M + i * HALO) * 4, value)

        @pl.loop(0, M // 2 // PAIRS)
        def _(t):
            for u in range(PAIRS):
                at = pl.ds(pl.multiple_of((t * PAIRS + u) * 8, 8), 8)
                here = recv[at, :]
                total = None
                for k in range(DEG):
                    a = src_s[t * (2 * PAIRS) + (k * M + 2 * u)]
                    b = src_s[t * (2 * PAIRS) + (k * M + 2 * u + 1)]
                    h = jnp.where(low, table[pl.ds(a, 8), :], table[pl.ds(b, 8), :]) + here
                    s = half_silu(h)
                    total = s if total is None else total + s
                sums[at, :] = total

        for k in range(M // CHUNK):
            rows = slice(k * CHUNK, (k + 1) * CHUNK)
            for j in range(D // TILE):
                esum[rows, j * TILE : (j + 1) * TILE] = sums[pl.ds(k * CHUNK * 4 + j, CHUNK, stride=4), :].astype(BF16)
            hidden = half_silu((up[rows, :] + dot(esum[rows, :], wup[layer, D : 2 * D, :])) * 0.5).astype(BF16)
            mixed = dot(hidden, wdown[layer])
            centre = mixed - jnp.mean(mixed, axis=1, keepdims=True)
            spread = jnp.mean(centre * centre, axis=1, keepdims=True)
            normed = centre * lax.rsqrt(spread + 1e-05) * gain[pl.ds(layer, 1), :]
            ext[rows, :] = (ext[rows, :].astype(F32) + normed).astype(BF16)

    result = pltpu.make_async_copy(ext, out_hbm, out_sem)
    result.start()
    result.wait()
    sent = inbox.at[pl.ds(0, OWNERS - 1)]
    pltpu.make_async_copy(sent, sent, send_sem.at[0]).wait()


def on_device(
    grid_feat, w_embed, w_send, edge_vec, g2m_sender, g2m_weight, g2m_target, w_agg, halo_rows, mesh_src,
    w_src, w_dst, w_up, w_down, ln_gain,
):
    args = (
        grid_feat.T, w_embed, w_send, edge_vec.reshape(1, D), g2m_sender.reshape(32, TILE), g2m_weight.reshape(32, TILE),
        g2m_target.reshape(32, TILE), w_agg, halo_rows.reshape(4, HALO), mesh_src.T, w_src, w_dst, w_up, w_down, ln_gain,
    )
    VM = pltpu.VMEM
    staged = [VM(a.shape, a.dtype) for a in args]
    scratch = [
        VM((W, GRID), BF16),
        VM((W, 2 * D), BF16),
        VM((8 * TILE, GRID), BF16),
        VM((32, TILE, W), BF16),
        VM((OWNERS, SLOTS, W), BF16),
        VM((M, 4 * CHUNK), BF16),
        VM((4 * CHUNK, D), BF16),
        VM((M, D), F32),
        VM((M, D), BF16),
        VM((4 * HALO, M), BF16),
        VM((LAYERS, 4 * HALO, D), BF16),
        VM((LAYERS, 4 * HALO, D), BF16),
        VM(((M + 4 * HALO) * 4 + 16, TILE), F32),
        VM((M * 4, TILE), F32),
        VM((M * 4, TILE), F32),
        VM((M, D), BF16),
        VM((M, D), F32),
        VM((DEG * M,), jnp.int32),
        pltpu.SMEM((DEG * M,), jnp.int32),
        pltpu.SemaphoreType.DMA((len(args),)),
        pltpu.SemaphoreType.DMA,
        pltpu.SemaphoreType.DMA((1,)),
        pltpu.SemaphoreType.DMA((16,)),
        pltpu.SemaphoreType.DMA((LAYERS, 4)),
        pltpu.SemaphoreType.DMA((LAYERS, 4)),
        pltpu.SemaphoreType.DMA,
        pltpu.SemaphoreType.REGULAR,
    ]
    anywhere = pl.BlockSpec(memory_space=pl.ANY)
    return pl.pallas_call(
        kernel,
        out_shape=jax.ShapeDtypeStruct((M, D), BF16),
        in_specs=[anywhere] * len(args),
        out_specs=anywhere,
        scratch_shapes=staged + scratch,
        compiler_params=pltpu.CompilerParams(collective_id=0, has_side_effects=True, vmem_limit_bytes=56 * 2**20),
    )(*args)


def solution(mesh):
    split = P(("band", "patch"), None)
    return jax.shard_map(
        on_device,
        mesh=mesh,
        in_specs=(
            split, P(), P(), P(), split, split, split, P(), P(("band", "patch"), None, None), split,
            P(), P(), P(), P(), P(),
        ),
        out_specs=split,
        check_vma=False,
    )
```

```python
import jax
import jax.numpy as jnp
from jax import lax
from jax.experimental import pallas as pl
from jax.experimental.pallas import tpu as pltpu
from jax.sharding import PartitionSpec as P

MESH = pl.DeviceIdType.MESH
BF16 = jnp.bfloat16
F32 = jnp.float32
VARS, D, W = 227, 512, 256
GRID, M, SLOTS, OWNERS = 2048, 1024, 32, 128
HALO, DEG, LAYERS = 128, 6, 2
TILE = 128
CHUNK = 256
PAIRS = 16


def dot(a, b):
    return jnp.dot(a, b, preferred_element_type=F32)


def half_silu(h):
    return h + h * jnp.tanh(h)


def column(row):
    return jnp.transpose(jnp.broadcast_to(row, (TILE, TILE)))


def lanes(shape):
    return lax.broadcasted_iota(jnp.int32, shape, len(shape) - 1)


def put_rows(ref, at, value):
    rows = value.shape[0]
    for j in range(D // TILE):
        ref[pl.ds(at + j, rows, stride=4), :] = value[:, j * TILE : (j + 1) * TILE]


def kernel(
    feat_hbm, embed_hbm, send_hbm, vec_hbm, sender_hbm, length_hbm, target_hbm, agg_hbm, halo_hbm, src_hbm,
    wsrc_hbm, wdst_hbm, wup_hbm, wdown_hbm, gain_hbm,
    out_hbm,
    feat, embed, wsend, vec, sender, length, target, wagg, halo_ids, src, wsrc, wdst, wup, wdown, gain,
    feat_pad, wcat, pick, outbox, inbox, turned, scatter, msgs, summed, ext, halo_pick, halo_out, halo_in,
    table, recv, sums, esum, up, src_v, src_s,
    in_sem, idx_sem, send_sem, recv_sem, halo_send, halo_recv, out_sem, ready,
):
    band, z = lax.axis_index("band"), lax.axis_index("patch")
    x, y, core = band // 8, (band // 2) % 4, band % 2

    def loads():
        pairs = (
            (sender_hbm, sender), (feat_hbm, feat), (length_hbm, length), (embed_hbm, embed), (vec_hbm, vec),
            (target_hbm, target), (src_hbm, src), (halo_hbm, halo_ids), (send_hbm, wsend), (agg_hbm, wagg),
            (wsrc_hbm, wsrc), (wdst_hbm, wdst), (wup_hbm, wup), (wdown_hbm, wdown), (gain_hbm, gain),
        )
        return [pltpu.make_async_copy(a, b, in_sem.at[i]) for i, (a, b) in enumerate(pairs)]

    plane = [((((x + i) % 4) * 4 + (y + j) % 4) * 2 + core, z) for i in range(4) for j in range(4) if i or j]
    line = [(band // 2 * 2 + (core + i) % 2, (z + j) % 4) for i in range(2) for j in range(4) if i or j]
    barrier = pltpu.get_barrier_semaphore()
    for device in plane + line:
        pl.semaphore_signal(barrier, inc=1, device_id=device, device_id_type=MESH)

    copies = loads()
    for copy in copies:
        copy.start()

    def pick_window(w):
        def band_of(i, j):
            return ((x + i) % 4 * 4 + (y + i + w) % 4) * 2 + (core + j) % 2

        for i in range(4):
            for j in range(2):
                ids = column(sender[pl.ds(band_of(i, j), 1), :])
                rows = slice((i * 2 + j) * TILE, (i * 2 + j + 1) * TILE)
                for k in range(GRID // TILE):
                    hit = ids == lanes((TILE, TILE)) + k * TILE
                    pick[rows, k * TILE : (k + 1) * TILE] = hit.astype(F32).astype(BF16)

    def rows_window(w):
        for i in range(4):
            both = lax.dot_general(
                pick[i * 2 * TILE : (i + 1) * 2 * TILE, :], feat_pad[...], (((1,), (1,)), ((), ())),
                preferred_element_type=F32,
            )
            for j in range(2):
                to = ((x + i) % 4 * 4 + (y + i + w) % 4) * 2 + (core + j) % 2
                rows = both[j * TILE : (j + 1) * TILE, :]
                long = column(length[pl.ds(to, 1), :])
                first = long.astype(BF16).astype(F32)
                second = (long - first).astype(BF16).astype(F32)
                third = long - first - second
                lane = lanes((TILE, TILE)) + TILE
                tail = rows[:, TILE:]
                tail = jnp.where(lane == VARS, first, tail)
                tail = jnp.where(lane == VARS + 1, second, tail)
                tail = jnp.where(lane == VARS + 2, third, tail)
                outbox[to, :, 0:TILE] = rows[:, :TILE].astype(BF16)
                outbox[to, :, TILE:W] = tail.astype(BF16)

    def send_window(w):
        for dz in range(4):
            for i in range(4):
                for j in range(2):
                    to = ((x + i) % 4 * 4 + (y + i + w) % 4) * 2 + (core + j) % 2
                    to_z = (z + dz) % 4
                    part = outbox.at[to, pl.ds(pl.multiple_of(to_z * SLOTS, SLOTS), SLOTS)]

                    def remote():
                        pltpu.make_async_remote_copy(
                            src_ref=part, dst_ref=inbox.at[w * 4 + dz, i * 2 + j], send_sem=send_sem.at[0],
                            recv_sem=recv_sem.at[w * 4 + dz], device_id=(to, to_z), device_id_type=MESH,
                        ).start()

                    if i == 0 and j == 0 and dz == 0:
                        pl.when(w != 0)(remote)

                        @pl.when(w == 0)
                        def _():
                            pltpu.make_async_copy(part, inbox.at[0, 0], recv_sem.at[0]).start()
                    else:
                        remote()

    copies[0].wait()
    pick_window(0)
    feat_pad[W - 32 : W, :] = jnp.zeros((32, GRID), BF16)
    copies[1].wait()
    copies[2].wait()
    feat_pad[0:VARS, :] = feat[...]
    pl.semaphore_wait(barrier, len(plane) + len(line))
    for device in line:
        pl.semaphore_signal(ready, inc=1, device_id=device, device_id_type=MESH)
    rows_window(0)
    pl.semaphore_wait(ready, len(line))
    send_window(0)

    @pl.loop(1, 4)
    def _(w):
        pick_window(w)
        rows_window(w)
        send_window(w)

    for copy in copies[3:]:
        copy.wait()
    wcat[...] = jnp.zeros((W, 2 * D), BF16)
    wcat[0:VARS, 0:D] = (embed[...].astype(F32) * 0.5).astype(BF16)
    edge_row = jnp.broadcast_to((vec[...].astype(F32) * 0.5)[None, :], (3, D)).astype(BF16)
    wcat[VARS : VARS + 3, D : 2 * D] = edge_row
    parity = (lanes((1, TILE)) + 1) % 2 * 4 + 4
    for k in range(DEG):
        for j in range(M // TILE):
            ids = src[k : k + 1, j * TILE : (j + 1) * TILE] * 4 + parity
            src_v[pl.ds(k * M + j * TILE, TILE)] = ids.reshape(TILE)
    src_copy = pltpu.make_async_copy(src_v, src_s, idx_sem)
    src_copy.start()
    for i in range(4):
        ids = column(halo_ids[i : i + 1, :])
        for k in range(M // TILE):
            hit = ids == lanes((TILE, TILE)) + k * TILE
            halo_pick[i * TILE : (i + 1) * TILE, k * TILE : (k + 1) * TILE] = hit.astype(F32).astype(BF16)
    summed[...] = jnp.zeros((M, D), F32)
    ends = (M + 4 * HALO) * 4 + 8
    table[0:8, :] = jnp.zeros((8, TILE), F32)
    table[ends : ends + 8, :] = jnp.zeros((8, TILE), F32)

    for q in range(4):
        turned[q] = pltpu.roll(target[...], (4 - z + q) % 4 * SLOTS, 1)

    def scatter_part(w, dz):
        back = (4 - dz) % 4
        block = lanes((1, TILE)) // SLOTS
        for h in range(2):
            ids = None
            for p in range(4):
                i, j = (h * 4 + p) // 2, p % 2
                source = ((x + 4 - i) % 4 * 4 + (y + 8 - i - w) % 4) * 2 + (core + j) % 2
                row = turned[(p - back) % 4, pl.ds(source, 1), :]
                ids = row if ids is None else jnp.where(block == p, row, ids)
            ids = jnp.broadcast_to(ids, (TILE, TILE))
            at = dz * CHUNK + h * TILE
            for k in range(M // TILE):
                hit = ids == lax.broadcasted_iota(jnp.int32, (TILE, TILE), 0) + k * TILE
                scatter[k * TILE : (k + 1) * TILE, at : at + TILE] = hit.astype(F32).astype(BF16)

    def messages_part(w, dz):
        part = inbox.at[w * 4 + dz]
        pltpu.make_async_copy(part, part, recv_sem.at[w * 4 + dz]).wait()
        first = dot(part[...].reshape(CHUNK, W), wcat[...])
        latent = half_silu(first[:, :D]).astype(BF16)
        pre = dot(latent, wsend[...]) * 0.5 + first[:, D:]
        msgs[dz * CHUNK : (dz + 1) * CHUNK, :] = half_silu(pre).astype(BF16)

    def add_parts(lo, hi):
        for k in range(M // CHUNK):
            rows = slice(k * CHUNK, (k + 1) * CHUNK)
            summed[rows, :] += dot(scatter[rows, lo * CHUNK : hi * CHUNK], msgs[lo * CHUNK : hi * CHUNK, :])

    @pl.loop(0, 3)
    def _(w):
        for dz in range(4):
            scatter_part(w, dz)
        for dz in range(4):
            messages_part(w, dz)
        add_parts(0, 4)

    for dz in range(4):
        scatter_part(3, dz)
    for dz in range(4):
        messages_part(3, dz)
        add_parts(dz, dz + 1)

    for k in range(M // CHUNK):
        rows = slice(k * CHUNK, (k + 1) * CHUNK)
        ext[rows, :] = half_silu(dot(summed[rows, :].astype(BF16), wagg[...]) * 0.5).astype(BF16)
    src_copy.wait()

    neighbours = ((band, (z + 1) % 4), (band, (z + 3) % 4), ((band + 1) % 32, z), ((band + 31) % 32, z))
    low = lax.broadcasted_iota(jnp.int32, (8, TILE), 0) < 4

    @pl.loop(0, LAYERS)
    def _(layer):
        halos = []
        for i in range(4):
            rows = slice(i * HALO, (i + 1) * HALO)
            if i % 2 == 0:
                both = slice(i * HALO, (i + 2) * HALO)
                halo_out[layer, both, :] = dot(halo_pick[both, :], ext[...]).astype(BF16)
            copy = pltpu.make_async_remote_copy(
                src_ref=halo_out.at[layer, rows], dst_ref=halo_in.at[layer, rows],
                send_sem=halo_send.at[layer, i], recv_sem=halo_recv.at[layer, i],
                device_id=neighbours[i], device_id_type=MESH,
            )
            copy.start()
            halos.append(copy)
        for k in range(M // CHUNK):
            rows = slice(k * CHUNK, (k + 1) * CHUNK)
            own = ext[rows, :]
            put_rows(table, 8 + k * CHUNK * 4, dot(own, wsrc[layer]) * 0.5)
            put_rows(recv, k * CHUNK * 4, dot(own, wdst[layer]) * 0.5)
            up[rows, :] = dot(own, wup[layer, 0:D, :])
        for i in range(4):
            halos[i].wait()
            rows = slice(i * HALO, (i + 1) * HALO)
            value = dot(halo_in[layer, rows, :], wsrc[layer]) * 0.5
            if i == 2:
                value = jnp.where(band == 0, 0.0, value)
            if i == 3:
                value = jnp.where(band == 31, 0.0, value)
            put_rows(table, 8 + (M + i * HALO) * 4, value)

        @pl.loop(0, M // 2 // PAIRS)
        def _(t):
            for u in range(PAIRS):
                at = pl.ds(pl.multiple_of((t * PAIRS + u) * 8, 8), 8)
                here = recv[at, :]
                total = None
                for k in range(DEG):
                    a = src_s.at[pl.ds(k * M + 2 * u, M - 2 * PAIRS + 1)][t * (2 * PAIRS)]
                    b = src_s.at[pl.ds(k * M + 2 * u + 1, M - 2 * PAIRS + 1)][t * (2 * PAIRS)]
                    h = jnp.where(low, table[pl.ds(a, 8), :], table[pl.ds(b, 8), :]) + here
                    s = half_silu(h)
                    total = s if total is None else total + s
                sums[at, :] = total

        for k in range(M // CHUNK):
            rows = slice(k * CHUNK, (k + 1) * CHUNK)
            for j in range(D // TILE):
                esum[rows, j * TILE : (j + 1) * TILE] = sums[pl.ds(k * CHUNK * 4 + j, CHUNK, stride=4), :].astype(BF16)
            hidden = half_silu((up[rows, :] + dot(esum[rows, :], wup[layer, D : 2 * D, :])) * 0.5).astype(BF16)
            mixed = dot(hidden, wdown[layer])
            centre = mixed - jnp.mean(mixed, axis=1, keepdims=True)
            spread = jnp.mean(centre * centre, axis=1, keepdims=True)
            normed = centre * lax.rsqrt(spread + 1e-05) * gain[pl.ds(layer, 1), :]
            ext[rows, :] = (ext[rows, :].astype(F32) + normed).astype(BF16)

    result = pltpu.make_async_copy(ext, out_hbm, out_sem)
    result.start()
    result.wait()
    for s in range(15):
        pltpu.make_async_copy(inbox.at[s], inbox.at[s], send_sem.at[0]).wait()
    sent = inbox.at[15, pl.ds(0, 7)]
    pltpu.make_async_copy(sent, sent, send_sem.at[0]).wait()


def on_device(
    grid_feat, w_embed, w_send, edge_vec, g2m_sender, g2m_weight, g2m_target, w_agg, halo_rows, mesh_src,
    w_src, w_dst, w_up, w_down, ln_gain,
):
    args = (
        grid_feat.T, w_embed, w_send, edge_vec, g2m_sender.reshape(32, TILE), g2m_weight.reshape(32, TILE),
        g2m_target.reshape(32, TILE), w_agg, halo_rows.reshape(4, HALO), mesh_src.T, w_src, w_dst, w_up, w_down, ln_gain,
    )
    VM = pltpu.VMEM
    staged = [VM(a.shape, a.dtype) for a in args]
    scratch = [
        VM((W, GRID), BF16),
        VM((W, 2 * D), BF16),
        VM((8 * TILE, GRID), BF16),
        VM((32, TILE, W), BF16),
        VM((16, 8, SLOTS, W), BF16),
        VM((4, 32, TILE), jnp.int32),
        VM((M, 4 * CHUNK), BF16),
        VM((4 * CHUNK, D), BF16),
        VM((M, D), F32),
        VM((M, D), BF16),
        VM((4 * HALO, M), BF16),
        VM((LAYERS, 4 * HALO, D), BF16),
        VM((LAYERS, 4 * HALO, D), BF16),
        VM(((M + 4 * HALO) * 4 + 16, TILE), F32),
        VM((M * 4, TILE), F32),
        VM((M * 4, TILE), F32),
        VM((M, D), BF16),
        VM((M, D), F32),
        VM((DEG * M,), jnp.int32),
        pltpu.SMEM((DEG * M,), jnp.int32),
        pltpu.SemaphoreType.DMA((len(args),)),
        pltpu.SemaphoreType.DMA,
        pltpu.SemaphoreType.DMA((1,)),
        pltpu.SemaphoreType.DMA((16,)),
        pltpu.SemaphoreType.DMA((LAYERS, 4)),
        pltpu.SemaphoreType.DMA((LAYERS, 4)),
        pltpu.SemaphoreType.DMA,
        pltpu.SemaphoreType.REGULAR,
    ]
    anywhere = pl.BlockSpec(memory_space=pl.ANY)
    return pl.pallas_call(
        kernel,
        out_shape=jax.ShapeDtypeStruct((M, D), BF16),
        in_specs=[anywhere] * len(args),
        out_specs=anywhere,
        scratch_shapes=staged + scratch,
        compiler_params=pltpu.CompilerParams(collective_id=0, has_side_effects=True, vmem_limit_bytes=56 * 2**20),
    )(*args)


def solution(mesh):
    split = P(("band", "patch"), None)
    return jax.shard_map(
        on_device,
        mesh=mesh,
        in_specs=(
            split, P(), P(), P(), split, split, split, P(), P(("band", "patch"), None, None), split,
            P(), P(), P(), P(), P(),
        ),
        out_specs=split,
        check_vma=False,
    )
```

```python
import jax
import jax.numpy as jnp
from jax import lax
from jax.experimental import pallas as pl
from jax.experimental.pallas import tpu as pltpu
from jax.sharding import PartitionSpec as P

MESH = pl.DeviceIdType.MESH
BF16 = jnp.bfloat16
F32 = jnp.float32
VARS, D, W = 227, 512, 256
GRID, M, SLOTS = 2048, 1024, 32
HALO, DEG, LAYERS = 128, 6, 2
TILE = 128
CHUNK = 256
PAIRS = 16
AHEAD = 6


def dot(a, b):
    return jnp.dot(a, b, preferred_element_type=F32)


def half_silu(h):
    return h + h * jnp.tanh(h)


def column(row):
    return jnp.transpose(jnp.broadcast_to(row, (TILE, TILE)))


def lanes(shape):
    return lax.broadcasted_iota(jnp.int32, shape, len(shape) - 1)


def put_rows(ref, at, value):
    rows = value.shape[0]
    for j in range(D // TILE):
        ref[pl.ds(at + j, rows, stride=4), :] = value[:, j * TILE : (j + 1) * TILE]


def kernel(
    feat_hbm, embed_hbm, send_hbm, vec_hbm, sender_hbm, length_hbm, target_hbm, agg_hbm, halo_hbm, src_hbm,
    wsrc_hbm, wdst_hbm, wup_hbm, wdown_hbm, gain_hbm,
    out_hbm,
    feat, embed, wsend, vec, sender, length, target, wagg, halo_ids, src, wsrc, wdst, wup, wdown, gain,
    feat_pad, wcat, pick, outbox, inbox, sender_turned, length_turned, target_turned, scatter, msgs, summed, ext, halo_pick, halo_out, halo_in,
    table, recv, sums, esum, up, src_v, src_s,
    in_sem, idx_sem, send_sem, recv_sem, halo_send, halo_recv, out_sem, ready,
):
    band, z = lax.axis_index("band"), lax.axis_index("patch")
    x, y, core = band // 8, (band // 2) % 4, band % 2

    def loads():
        pairs = (
            (sender_hbm, sender), (feat_hbm, feat), (length_hbm, length), (embed_hbm, embed), (vec_hbm, vec),
            (target_hbm, target), (src_hbm, src), (halo_hbm, halo_ids), (send_hbm, wsend), (agg_hbm, wagg),
            (wsrc_hbm, wsrc), (wdst_hbm, wdst), (wup_hbm, wup), (wdown_hbm, wdown), (gain_hbm, gain),
        )
        return [pltpu.make_async_copy(a, b, in_sem.at[i]) for i, (a, b) in enumerate(pairs)]

    plane = [((((x + i) % 4) * 4 + (y + j) % 4) * 2 + core, z) for i in range(4) for j in range(4) if i or j]
    line = [(band // 2 * 2 + (core + i) % 2, (z + j) % 4) for i in range(2) for j in range(4) if i or j]
    barrier = pltpu.get_barrier_semaphore()
    for device in plane + line:
        pl.semaphore_signal(barrier, inc=1, device_id=device, device_id_type=MESH)

    copies = loads()
    for copy in copies:
        copy.start()

    block = lanes((1, TILE)) // SLOTS

    def sign(piece, way):
        return 1 - 2 * core if way == 1 else 2 * ((core + piece % 2) % 2) - 1

    def band_at(part, piece, way):
        i, j, w = piece // 2, piece % 2, part // 4
        s = sign(piece, way)
        return ((x + 4 + s * i) % 4 * 4 + (y + 8 + s * (i + w)) % 4) * 2 + (core + j) % 2

    def z_at(part, piece, way):
        return (z + 4 + sign(piece, way) * (part % 4)) % 4

    def turn(ref, turned):
        for q in range(4):
            turned[q] = pltpu.roll(ref[...], (4 - z + q) % 4 * SLOTS, 1)

    def pieces(turned, part, half, way):
        row = None
        for p in range(4):
            got = turned[(p + 4 + z - z_at(part, p, way)) % 4, pl.ds(band_at(part, half * 4 + p, way), 1), :]
            row = got if row is None else jnp.where(block == p, got, row)
        return row

    def gather_part(part):
        for half in range(2):
            ids = column(pieces(sender_turned, part, half, 1))
            for k in range(GRID // TILE):
                hit = ids == lanes((TILE, TILE)) + k * TILE
                pick[half * TILE : (half + 1) * TILE, k * TILE : (k + 1) * TILE] = hit.astype(F32).astype(BF16)
        both = lax.dot_general(
            pick[...], feat_pad[...], (((1,), (1,)), ((), ())), preferred_element_type=F32
        )
        for half in range(2):
            rows = both[half * TILE : (half + 1) * TILE, :]
            long = column(pieces(length_turned, part, half, 1))
            first = long.astype(BF16).astype(F32)
            second = (long - first).astype(BF16).astype(F32)
            third = long - first - second
            lane = lanes((TILE, TILE)) + TILE
            tail = rows[:, TILE:]
            tail = jnp.where(lane == VARS, first, tail)
            tail = jnp.where(lane == VARS + 1, second, tail)
            tail = jnp.where(lane == VARS + 2, third, tail)
            to = slice(half * TILE, (half + 1) * TILE)
            outbox[part, to, 0:TILE] = rows[:, :TILE].astype(BF16)
            outbox[part, to, TILE:W] = tail.astype(BF16)

    def send_part(part):
        to_z = z_at(part, 0, 1)
        for piece in range(8):
            rows = outbox.at[part, pl.ds(piece * SLOTS, SLOTS)]
            there = inbox.at[part, pl.ds(piece * SLOTS, SLOTS)]

            def remote():
                pltpu.make_async_remote_copy(
                    src_ref=rows, dst_ref=there, send_sem=send_sem.at[part], recv_sem=recv_sem.at[part],
                    device_id=(band_at(part, piece, 1), to_z), device_id_type=MESH,
                ).start()

            if piece == 0:
                pl.when(part != 0)(remote)

                @pl.when(part == 0)
                def _():
                    pltpu.make_async_copy(rows, there, recv_sem.at[part]).start()
            else:
                remote()

    def wait_sent(part):
        @pl.when(part == 0)
        def _():
            rows = inbox.at[0, pl.ds(0, 7 * SLOTS)]
            pltpu.make_async_copy(rows, rows, send_sem.at[0]).wait()

        @pl.when(part != 0)
        def _():
            pltpu.make_async_copy(inbox.at[part], inbox.at[part], send_sem.at[part]).wait()

    pl.semaphore_wait(barrier, len(plane) + len(line))
    for device in line:
        pl.semaphore_signal(ready, inc=1, device_id=device, device_id_type=MESH)
    feat_pad[W - 32 : W, :] = jnp.zeros((32, GRID), BF16)
    copies[0].wait()
    turn(sender, sender_turned)
    copies[2].wait()
    turn(length, length_turned)
    copies[1].wait()
    feat_pad[0:VARS, :] = feat[...]
    gather_part(0)
    pl.semaphore_wait(ready, len(line))
    send_part(0)

    @pl.loop(1, AHEAD)
    def _(part):
        gather_part(part)
        send_part(part)

    for copy in copies[3:]:
        copy.wait()
    wcat[...] = jnp.zeros((W, 2 * D), BF16)
    wcat[0:VARS, 0:D] = (embed[...].astype(F32) * 0.5).astype(BF16)
    edge_row = jnp.broadcast_to((vec[...].astype(F32) * 0.5)[None, :], (3, D)).astype(BF16)
    wcat[VARS : VARS + 3, D : 2 * D] = edge_row
    parity = (lanes((1, TILE)) + 1) % 2 * 4 + 4
    for k in range(DEG):
        for j in range(M // TILE):
            ids = src[k : k + 1, j * TILE : (j + 1) * TILE] * 4 + parity
            src_v[pl.ds(k * M + j * TILE, TILE)] = ids.reshape(TILE)
    src_copy = pltpu.make_async_copy(src_v, src_s, idx_sem)
    src_copy.start()
    for i in range(4):
        ids = column(halo_ids[i : i + 1, :])
        for k in range(M // TILE):
            hit = ids == lanes((TILE, TILE)) + k * TILE
            halo_pick[i * TILE : (i + 1) * TILE, k * TILE : (k + 1) * TILE] = hit.astype(F32).astype(BF16)
    turn(target, target_turned)
    summed[...] = jnp.zeros((M, D), F32)
    ends = (M + 4 * HALO) * 4 + 8
    table[0:8, :] = jnp.zeros((8, TILE), F32)
    table[ends : ends + 8, :] = jnp.zeros((8, TILE), F32)

    @pl.loop(0, 16)
    def _(part):
        wait_sent(part)

        @pl.when(part + AHEAD < 16)
        def _():
            gather_part(part + AHEAD)
            send_part(part + AHEAD)

        for half in range(2):
            ids = jnp.broadcast_to(pieces(target_turned, part, half, -1), (TILE, TILE))
            for k in range(M // TILE):
                hit = ids == lax.broadcasted_iota(jnp.int32, (TILE, TILE), 0) + k * TILE
                scatter[k * TILE : (k + 1) * TILE, half * TILE : (half + 1) * TILE] = hit.astype(F32).astype(BF16)
        pltpu.make_async_copy(inbox.at[part], inbox.at[part], recv_sem.at[part]).wait()
        first = dot(inbox[part], wcat[...])
        latent = half_silu(first[:, :D]).astype(BF16)
        pre = dot(latent, wsend[...]) * 0.5 + first[:, D:]
        msgs[...] = half_silu(pre).astype(BF16)
        for k in range(M // CHUNK):
            rows = slice(k * CHUNK, (k + 1) * CHUNK)
            summed[rows, :] += dot(scatter[rows, :], msgs[...])

    for k in range(M // CHUNK):
        rows = slice(k * CHUNK, (k + 1) * CHUNK)
        ext[rows, :] = half_silu(dot(summed[rows, :].astype(BF16), wagg[...]) * 0.5).astype(BF16)
    src_copy.wait()

    neighbours = ((band, (z + 1) % 4), (band, (z + 3) % 4), ((band + 1) % 32, z), ((band + 31) % 32, z))
    low = lax.broadcasted_iota(jnp.int32, (8, TILE), 0) < 4

    @pl.loop(0, LAYERS)
    def _(layer):
        halos = []
        for i in range(4):
            rows = slice(i * HALO, (i + 1) * HALO)
            if i % 2 == 0:
                both = slice(i * HALO, (i + 2) * HALO)
                halo_out[layer, both, :] = dot(halo_pick[both, :], ext[...]).astype(BF16)
            copy = pltpu.make_async_remote_copy(
                src_ref=halo_out.at[layer, rows], dst_ref=halo_in.at[layer, rows],
                send_sem=halo_send.at[layer, i], recv_sem=halo_recv.at[layer, i],
                device_id=neighbours[i], device_id_type=MESH,
            )
            copy.start()
            halos.append(copy)
        for k in range(M // CHUNK):
            rows = slice(k * CHUNK, (k + 1) * CHUNK)
            own = ext[rows, :]
            put_rows(table, 8 + k * CHUNK * 4, dot(own, wsrc[layer]) * 0.5)
            put_rows(recv, k * CHUNK * 4, dot(own, wdst[layer]) * 0.5)
            up[rows, :] = dot(own, wup[layer, 0:D, :])
        for i in range(4):
            halos[i].wait()
            rows = slice(i * HALO, (i + 1) * HALO)
            value = dot(halo_in[layer, rows, :], wsrc[layer]) * 0.5
            if i == 2:
                value = jnp.where(band == 0, 0.0, value)
            if i == 3:
                value = jnp.where(band == 31, 0.0, value)
            put_rows(table, 8 + (M + i * HALO) * 4, value)

        @pl.loop(0, M // 2 // PAIRS)
        def _(t):
            for u in range(PAIRS):
                at = pl.ds(pl.multiple_of((t * PAIRS + u) * 8, 8), 8)
                here = recv[at, :]
                total = None
                for k in range(DEG):
                    a = src_s.at[pl.ds(k * M + 2 * u, M - 2 * PAIRS + 1)][t * (2 * PAIRS)]
                    b = src_s.at[pl.ds(k * M + 2 * u + 1, M - 2 * PAIRS + 1)][t * (2 * PAIRS)]
                    h = jnp.where(low, table[pl.ds(a, 8), :], table[pl.ds(b, 8), :]) + here
                    s = half_silu(h)
                    total = s if total is None else total + s
                sums[at, :] = total

        for k in range(M // CHUNK):
            rows = slice(k * CHUNK, (k + 1) * CHUNK)
            for j in range(D // TILE):
                esum[rows, j * TILE : (j + 1) * TILE] = sums[pl.ds(k * CHUNK * 4 + j, CHUNK, stride=4), :].astype(BF16)
            hidden = half_silu((up[rows, :] + dot(esum[rows, :], wup[layer, D : 2 * D, :])) * 0.5).astype(BF16)
            mixed = dot(hidden, wdown[layer])
            centre = mixed - jnp.mean(mixed, axis=1, keepdims=True)
            spread = jnp.mean(centre * centre, axis=1, keepdims=True)
            normed = centre * lax.rsqrt(spread + 1e-05) * gain[pl.ds(layer, 1), :]
            ext[rows, :] = (ext[rows, :].astype(F32) + normed).astype(BF16)

    result = pltpu.make_async_copy(ext, out_hbm, out_sem)
    result.start()
    result.wait()


def on_device(
    grid_feat, w_embed, w_send, edge_vec, g2m_sender, g2m_weight, g2m_target, w_agg, halo_rows, mesh_src,
    w_src, w_dst, w_up, w_down, ln_gain,
):
    args = (
        grid_feat.T, w_embed, w_send, edge_vec, g2m_sender.reshape(32, TILE), g2m_weight.reshape(32, TILE),
        g2m_target.reshape(32, TILE), w_agg, halo_rows.reshape(4, HALO), mesh_src.T, w_src, w_dst, w_up, w_down, ln_gain,
    )
    VM = pltpu.VMEM
    staged = [VM(a.shape, a.dtype) for a in args]
    scratch = [
        VM((W, GRID), BF16),
        VM((W, 2 * D), BF16),
        VM((CHUNK, GRID), BF16),
        VM((16, CHUNK, W), BF16),
        VM((16, CHUNK, W), BF16),
        VM((4, 32, TILE), jnp.int32),
        VM((4, 32, TILE), F32),
        VM((4, 32, TILE), jnp.int32),
        VM((M, CHUNK), BF16),
        VM((CHUNK, D), BF16),
        VM((M, D), F32),
        VM((M, D), BF16),
        VM((4 * HALO, M), BF16),
        VM((LAYERS, 4 * HALO, D), BF16),
        VM((LAYERS, 4 * HALO, D), BF16),
        VM(((M + 4 * HALO) * 4 + 16, TILE), F32),
        VM((M * 4, TILE), F32),
        VM((M * 4, TILE), F32),
        VM((M, D), BF16),
        VM((M, D), F32),
        VM((DEG * M,), jnp.int32),
        pltpu.SMEM((DEG * M,), jnp.int32),
        pltpu.SemaphoreType.DMA((len(args),)),
        pltpu.SemaphoreType.DMA,
        pltpu.SemaphoreType.DMA((16,)),
        pltpu.SemaphoreType.DMA((16,)),
        pltpu.SemaphoreType.DMA((LAYERS, 4)),
        pltpu.SemaphoreType.DMA((LAYERS, 4)),
        pltpu.SemaphoreType.DMA,
        pltpu.SemaphoreType.REGULAR,
    ]
    anywhere = pl.BlockSpec(memory_space=pl.ANY)
    return pl.pallas_call(
        kernel,
        out_shape=jax.ShapeDtypeStruct((M, D), BF16),
        in_specs=[anywhere] * len(args),
        out_specs=anywhere,
        scratch_shapes=staged + scratch,
        compiler_params=pltpu.CompilerParams(collective_id=0, has_side_effects=True, vmem_limit_bytes=56 * 2**20),
    )(*args)


def solution(mesh):
    split = P(("band", "patch"), None)
    return jax.shard_map(
        on_device,
        mesh=mesh,
        in_specs=(
            split, P(), P(), P(), split, split, split, P(), P(("band", "patch"), None, None), split,
            P(), P(), P(), P(), P(),
        ),
        out_specs=split,
        check_vma=False,
    )
```

```python
import jax
import jax.numpy as jnp
from jax import lax
from jax.experimental import pallas as pl
from jax.experimental.pallas import tpu as pltpu
from jax.sharding import PartitionSpec as P

MESH = pl.DeviceIdType.MESH
BF16 = jnp.bfloat16
F32 = jnp.float32
VARS, D, W = 227, 512, 256
GRID, M, SLOTS = 2048, 1024, 32
HALO, DEG, LAYERS = 128, 6, 2
TILE = 128
CHUNK = 256
PAIRS = 16
AHEAD = 6
STEP = 2


def dot(a, b):
    return jnp.dot(a, b, preferred_element_type=F32)


def half_silu(h):
    return h + h * jnp.tanh(h)


def column(row):
    return jnp.transpose(jnp.broadcast_to(row, (TILE, TILE)))


def lanes(shape):
    return lax.broadcasted_iota(jnp.int32, shape, len(shape) - 1)


def put_rows(ref, at, value):
    rows = value.shape[0]
    for j in range(D // TILE):
        ref[pl.ds(at + j, rows, stride=4), :] = value[:, j * TILE : (j + 1) * TILE]


def kernel(
    feat_hbm, embed_hbm, send_hbm, vec_hbm, sender_hbm, length_hbm, target_hbm, agg_hbm, halo_hbm, src_hbm,
    wsrc_hbm, wdst_hbm, wup_hbm, wdown_hbm, gain_hbm,
    out_hbm,
    feat, embed, wsend, vec, sender, length, target, wagg, halo_ids, src, wsrc, wdst, wup, wdown, gain,
    feat_pad, wcat, pick, outbox, inbox, sender_turned, length_turned, target_turned, scatter, msgs, summed, ext, halo_pick, halo_out, halo_in,
    halo_now, halo_up, table, recv, sums, esum, up, src_v, src_s,
    in_sem, idx_sem, send_sem, recv_sem, halo_send, halo_recv, out_sem, ready,
):
    band, z = lax.axis_index("band"), lax.axis_index("patch")
    x, y, core = band // 8, (band // 2) % 4, band % 2

    def loads():
        pairs = (
            (sender_hbm, sender), (feat_hbm, feat), (length_hbm, length), (embed_hbm, embed), (vec_hbm, vec),
            (target_hbm, target), (src_hbm, src), (halo_hbm, halo_ids), (send_hbm, wsend), (agg_hbm, wagg),
            (wsrc_hbm, wsrc), (wdst_hbm, wdst), (wup_hbm, wup), (wdown_hbm, wdown), (gain_hbm, gain),
        )
        return [pltpu.make_async_copy(a, b, in_sem.at[i]) for i, (a, b) in enumerate(pairs)]

    plane = [((((x + i) % 4) * 4 + (y + j) % 4) * 2 + core, z) for i in range(4) for j in range(4) if i or j]
    line = [(band // 2 * 2 + (core + i) % 2, (z + j) % 4) for i in range(2) for j in range(4) if i or j]
    barrier = pltpu.get_barrier_semaphore()
    for device in plane + line:
        pl.semaphore_signal(barrier, inc=1, device_id=device, device_id_type=MESH)

    copies = loads()
    for copy in copies:
        copy.start()

    block = lanes((1, TILE)) // SLOTS

    def sign(piece, way):
        return 1 - 2 * core if way == 1 else 2 * ((core + piece % 2) % 2) - 1

    def band_at(part, piece, way):
        i, j, w = piece // 2, piece % 2, part // 4
        s = sign(piece, way)
        return ((x + 4 + s * i) % 4 * 4 + (y + 8 + s * (i + w)) % 4) * 2 + (core + j) % 2

    def z_at(part, piece, way):
        return (z + 4 + sign(piece, way) * (part % 4)) % 4

    def turn(ref, turned):
        for q in range(4):
            turned[q] = pltpu.roll(ref[...], (4 - z + q) % 4 * SLOTS, 1)

    def pieces(turned, part, half, way):
        row = None
        for p in range(4):
            got = turned[(p + 4 + z - z_at(part, p, way)) % 4, pl.ds(band_at(part, half * 4 + p, way), 1), :]
            row = got if row is None else jnp.where(block == p, got, row)
        return row

    def gather_part(part):
        for half in range(2):
            ids = column(pieces(sender_turned, part, half, 1))
            for k in range(GRID // TILE):
                hit = ids == lanes((TILE, TILE)) + k * TILE
                pick[half * TILE : (half + 1) * TILE, k * TILE : (k + 1) * TILE] = hit.astype(F32).astype(BF16)
        both = lax.dot_general(
            pick[...], feat_pad[...], (((1,), (1,)), ((), ())), preferred_element_type=F32
        )
        for half in range(2):
            rows = both[half * TILE : (half + 1) * TILE, :]
            long = column(pieces(length_turned, part, half, 1))
            first = long.astype(BF16).astype(F32)
            second = (long - first).astype(BF16).astype(F32)
            third = long - first - second
            lane = lanes((TILE, TILE)) + TILE
            tail = rows[:, TILE:]
            tail = jnp.where(lane == VARS, first, tail)
            tail = jnp.where(lane == VARS + 1, second, tail)
            tail = jnp.where(lane == VARS + 2, third, tail)
            to = slice(half * TILE, (half + 1) * TILE)
            outbox[part, to, 0:TILE] = rows[:, :TILE].astype(BF16)
            outbox[part, to, TILE:W] = tail.astype(BF16)

    def send_part(part):
        to_z = z_at(part, 0, 1)
        for piece in range(8):
            rows = outbox.at[part, pl.ds(piece * SLOTS, SLOTS)]
            there = inbox.at[part, pl.ds(piece * SLOTS, SLOTS)]

            def remote():
                pltpu.make_async_remote_copy(
                    src_ref=rows, dst_ref=there, send_sem=send_sem.at[part], recv_sem=recv_sem.at[part],
                    device_id=(band_at(part, piece, 1), to_z), device_id_type=MESH,
                ).start()

            if piece == 0:
                pl.when(part != 0)(remote)

                @pl.when(part == 0)
                def _():
                    pltpu.make_async_copy(rows, there, recv_sem.at[part]).start()
            else:
                remote()

    def wait_sent(part):
        @pl.when(part == 0)
        def _():
            rows = inbox.at[0, pl.ds(0, 7 * SLOTS)]
            pltpu.make_async_copy(rows, rows, send_sem.at[0]).wait()

        @pl.when(part != 0)
        def _():
            pltpu.make_async_copy(inbox.at[part], inbox.at[part], send_sem.at[part]).wait()

    pl.semaphore_wait(barrier, len(plane) + len(line))
    for device in line:
        pl.semaphore_signal(ready, inc=1, device_id=device, device_id_type=MESH)
    feat_pad[W - 32 : W, :] = jnp.zeros((32, GRID), BF16)
    copies[0].wait()
    turn(sender, sender_turned)
    copies[2].wait()
    turn(length, length_turned)
    copies[1].wait()
    feat_pad[0:VARS, :] = feat[...]
    gather_part(0)
    pl.semaphore_wait(ready, len(line))
    send_part(0)

    @pl.loop(1, AHEAD)
    def _(part):
        gather_part(part)
        send_part(part)

    for copy in copies[3:]:
        copy.wait()
    wcat[...] = jnp.zeros((W, 2 * D), BF16)
    wcat[0:VARS, 0:D] = (embed[...].astype(F32) * 0.5).astype(BF16)
    edge_row = jnp.broadcast_to((vec[...].astype(F32) * 0.5)[None, :], (3, D)).astype(BF16)
    wcat[VARS : VARS + 3, D : 2 * D] = edge_row
    parity = (lanes((1, TILE)) + 1) % 2 * 4 + 4
    for k in range(DEG):
        for j in range(M // TILE):
            ids = src[k : k + 1, j * TILE : (j + 1) * TILE] * 4 + parity
            src_v[pl.ds(k * M + j * TILE, TILE)] = ids.reshape(TILE)
    src_copy = pltpu.make_async_copy(src_v, src_s, idx_sem)
    src_copy.start()
    for i in range(4):
        ids = column(halo_ids[i : i + 1, :])
        for k in range(M // TILE):
            hit = ids == lanes((TILE, TILE)) + k * TILE
            halo_pick[i * TILE : (i + 1) * TILE, k * TILE : (k + 1) * TILE] = hit.astype(F32).astype(BF16)
    turn(target, target_turned)
    summed[...] = jnp.zeros((M, D), F32)
    ends = (M + 4 * HALO) * 4 + 8
    table[0:8, :] = jnp.zeros((8, TILE), F32)
    table[ends : ends + 8, :] = jnp.zeros((8, TILE), F32)

    @pl.loop(0, 16 // STEP)
    def _(step):
        for h in range(STEP):
            wait_sent(step * STEP + h)

        @pl.when(step * STEP + AHEAD < 16)
        def _():
            @pl.loop(0, STEP)
            def _(h):
                gather_part(step * STEP + AHEAD + h)
                send_part(step * STEP + AHEAD + h)

        for h in range(STEP * 2):
            ids = jnp.broadcast_to(pieces(target_turned, step * STEP + h // 2, h % 2, -1), (TILE, TILE))
            for k in range(M // TILE):
                hit = ids == lax.broadcasted_iota(jnp.int32, (TILE, TILE), 0) + k * TILE
                scatter[k * TILE : (k + 1) * TILE, h * TILE : (h + 1) * TILE] = hit.astype(F32).astype(BF16)
        for h in range(STEP):
            part = step * STEP + h
            pltpu.make_async_copy(inbox.at[part], inbox.at[part], recv_sem.at[part]).wait()
        rows = inbox[pl.ds(step * STEP, STEP)].reshape(STEP * CHUNK, W)
        latent = half_silu(dot(rows, wcat[:, :D])).astype(BF16)
        pre = dot(latent, wsend[...]) * 0.5 + dot(rows[:, TILE:], wcat[TILE:, D:])
        msgs[...] = half_silu(pre).astype(BF16)
        for k in range(M // CHUNK):
            rows = slice(k * CHUNK, (k + 1) * CHUNK)
            summed[rows, :] += dot(scatter[rows, :], msgs[...])

    neighbours = ((band, (z + 1) % 4), (band, (z + 3) % 4), ((band + 1) % 32, z), ((band + 31) % 32, z))
    low = lax.broadcasted_iota(jnp.int32, (8, TILE), 0) < 4

    def send_halos(layer, values):
        copies = []
        for i in range(4):
            rows = slice(i * HALO, (i + 1) * HALO)
            if i % 2 == 0:
                both = slice(i * HALO, (i + 2) * HALO)
                halo_out[layer, both, :] = dot(halo_pick[both, :], values[...]).astype(BF16)
            copy = pltpu.make_async_remote_copy(
                src_ref=halo_out.at[layer, rows], dst_ref=halo_in.at[layer, rows],
                send_sem=halo_send.at[layer, i], recv_sem=halo_recv.at[layer, i],
                device_id=neighbours[i], device_id_type=MESH,
            )
            copy.start()
            copies.append(copy)
        return copies

    def aggregated(sums_16):
        return half_silu(dot(sums_16, wagg[...]) * 0.5).astype(BF16)

    def updated(layer, own, first, sums_16):
        hidden = half_silu((first + dot(sums_16, wup[layer, D : 2 * D, :])) * 0.5).astype(BF16)
        mixed = dot(hidden, wdown[layer])
        centre = mixed - jnp.mean(mixed, axis=1, keepdims=True)
        spread = jnp.mean(centre * centre, axis=1, keepdims=True)
        normed = centre * lax.rsqrt(spread + 1e-05) * gain[layer : layer + 1, :]
        return (own.astype(F32) + normed).astype(BF16)

    def project(layer):
        for k in range(M // CHUNK):
            rows = slice(k * CHUNK, (k + 1) * CHUNK)
            own = ext[rows, :]
            put_rows(table, 8 + k * CHUNK * 4, dot(own, wsrc[layer]) * 0.5)
            put_rows(recv, k * CHUNK * 4, dot(own, wdst[layer]) * 0.5)
            up[rows, :] = dot(own, wup[layer, 0:D, :])

    def edges():
        @pl.loop(0, M // 2 // PAIRS)
        def _(t):
            for u in range(PAIRS):
                at = pl.ds(pl.multiple_of((t * PAIRS + u) * 8, 8), 8)
                here = recv[at, :]
                total = None
                for k in range(DEG):
                    a = src_s.at[pl.ds(k * M + 2 * u, M - 2 * PAIRS + 1)][t * (2 * PAIRS)]
                    b = src_s.at[pl.ds(k * M + 2 * u + 1, M - 2 * PAIRS + 1)][t * (2 * PAIRS)]
                    h = jnp.where(low, table[pl.ds(a, 8), :], table[pl.ds(b, 8), :]) + here
                    s = half_silu(h)
                    total = s if total is None else total + s
                sums[at, :] = total

        for k in range(M // CHUNK):
            rows = slice(k * CHUNK, (k + 1) * CHUNK)
            for j in range(D // TILE):
                esum[rows, j * TILE : (j + 1) * TILE] = sums[pl.ds(k * CHUNK * 4 + j, CHUNK, stride=4), :].astype(BF16)

    def put_halo(layer, i, rows):
        value = dot(rows, wsrc[layer]) * 0.5
        if i == 2:
            value = jnp.where(band == 0, 0.0, value)
        if i == 3:
            value = jnp.where(band == 31, 0.0, value)
        put_rows(table, 8 + (M + i * HALO) * 4, value)

    esum[...] = summed[...].astype(BF16)
    halos = send_halos(0, esum)
    for k in range(M // CHUNK):
        rows = slice(k * CHUNK, (k + 1) * CHUNK)
        ext[rows, :] = aggregated(esum[rows, :])
    project(0)
    src_copy.wait()
    for i in (2, 3, 0, 1):
        rows = slice(i * HALO, (i + 1) * HALO)
        halos[i].wait()
        halo_now[rows, :] = aggregated(halo_in[0, rows, :])
        put_halo(0, i, halo_now[rows, :])
    edges()

    halos = send_halos(1, esum)
    for k in range(M // CHUNK):
        rows = slice(k * CHUNK, (k + 1) * CHUNK)
        ext[rows, :] = updated(0, ext[rows, :], up[rows, :], esum[rows, :])
    for k in range(2):
        rows = slice(k * CHUNK, (k + 1) * CHUNK)
        halo_up[rows, :] = dot(halo_now[rows, :], wup[0, 0:D, :])
    project(1)
    for i in (2, 3, 0, 1):
        rows = slice(i * HALO, (i + 1) * HALO)
        halos[i].wait()
        put_halo(1, i, updated(0, halo_now[rows, :], halo_up[rows, :], halo_in[1, rows, :]))
    edges()
    for k in range(M // CHUNK):
        rows = slice(k * CHUNK, (k + 1) * CHUNK)
        ext[rows, :] = updated(1, ext[rows, :], up[rows, :], esum[rows, :])
        pltpu.make_async_copy(ext.at[rows], out_hbm.at[rows], out_sem).start()
    pltpu.make_async_copy(ext, out_hbm, out_sem).wait()


def on_device(
    grid_feat, w_embed, w_send, edge_vec, g2m_sender, g2m_weight, g2m_target, w_agg, halo_rows, mesh_src,
    w_src, w_dst, w_up, w_down, ln_gain,
):
    args = (
        grid_feat.T, w_embed, w_send, edge_vec, g2m_sender.reshape(32, TILE), g2m_weight.reshape(32, TILE),
        g2m_target.reshape(32, TILE), w_agg, halo_rows.reshape(4, HALO), mesh_src.T, w_src, w_dst, w_up, w_down, ln_gain,
    )
    VM = pltpu.VMEM
    staged = [VM(a.shape, a.dtype) for a in args]
    scratch = [
        VM((W, GRID), BF16),
        VM((W, 2 * D), BF16),
        VM((CHUNK, GRID), BF16),
        VM((16, CHUNK, W), BF16),
        VM((16, CHUNK, W), BF16),
        VM((4, 32, TILE), jnp.int32),
        VM((4, 32, TILE), F32),
        VM((4, 32, TILE), jnp.int32),
        VM((M, STEP * CHUNK), BF16),
        VM((STEP * CHUNK, D), BF16),
        VM((M, D), F32),
        VM((M, D), BF16),
        VM((4 * HALO, M), BF16),
        VM((LAYERS, 4 * HALO, D), BF16),
        VM((LAYERS, 4 * HALO, D), BF16),
        VM((4 * HALO, D), BF16),
        VM((4 * HALO, D), F32),
        VM(((M + 4 * HALO) * 4 + 16, TILE), F32),
        VM((M * 4, TILE), F32),
        VM((M * 4, TILE), F32),
        VM((M, D), BF16),
        VM((M, D), F32),
        VM((DEG * M,), jnp.int32),
        pltpu.SMEM((DEG * M,), jnp.int32),
        pltpu.SemaphoreType.DMA((len(args),)),
        pltpu.SemaphoreType.DMA,
        pltpu.SemaphoreType.DMA((16,)),
        pltpu.SemaphoreType.DMA((16,)),
        pltpu.SemaphoreType.DMA((LAYERS, 4)),
        pltpu.SemaphoreType.DMA((LAYERS, 4)),
        pltpu.SemaphoreType.DMA,
        pltpu.SemaphoreType.REGULAR,
    ]
    anywhere = pl.BlockSpec(memory_space=pl.ANY)
    return pl.pallas_call(
        kernel,
        out_shape=jax.ShapeDtypeStruct((M, D), BF16),
        in_specs=[anywhere] * len(args),
        out_specs=anywhere,
        scratch_shapes=staged + scratch,
        compiler_params=pltpu.CompilerParams(collective_id=0, has_side_effects=True, vmem_limit_bytes=56 * 2**20),
    )(*args)


def solution(mesh):
    split = P(("band", "patch"), None)
    return jax.shard_map(
        on_device,
        mesh=mesh,
        in_specs=(
            split, P(), P(), P(), split, split, split, P(), P(("band", "patch"), None, None), split,
            P(), P(), P(), P(), P(),
        ),
        out_specs=split,
        check_vma=False,
    )
```

```python
import jax
import jax.numpy as jnp
from jax import lax
from jax.experimental import pallas as pl
from jax.experimental.pallas import tpu as pltpu
from jax.sharding import PartitionSpec as P

MESH = pl.DeviceIdType.MESH
BF16 = jnp.bfloat16
F32 = jnp.float32
VARS, D, W = 227, 512, 256
GRID, M, SLOTS = 2048, 1024, 32
HALO, DEG, LAYERS = 128, 6, 2
TILE = 128
CHUNK = 256
PAIRS = 16
AHEAD = 6
STEP = 2


def dot(a, b):
    return jnp.dot(a, b, preferred_element_type=F32)


def half_silu(h):
    return h + h * jnp.tanh(h)


def column(row):
    return jnp.transpose(jnp.broadcast_to(row, (TILE, TILE)))


def lanes(shape):
    return lax.broadcasted_iota(jnp.int32, shape, len(shape) - 1)


def put_rows(ref, at, value):
    rows = value.shape[0]
    for j in range(D // TILE):
        ref[pl.ds(at + j, rows, stride=4), :] = value[:, j * TILE : (j + 1) * TILE]


def kernel(
    feat_hbm, embed_hbm, send_hbm, vec_hbm, sender_hbm, length_hbm, target_hbm, agg_hbm, halo_hbm, src_hbm,
    wsrc_hbm, wdst_hbm, wup_hbm, wdown_hbm, gain_hbm,
    out_hbm,
    feat, embed, wsend, vec, sender, length, target, wagg, halo_ids, src, wsrc, wdst, wup, wdown, gain,
    feat_pad, wcat, pick, outbox, inbox, sender_turned, length_turned, target_turned, scatter, msgs, summed, ext, halo_pick, halo_out, halo_in,
    halo_now, halo_up, table, recv, sums, esum, up, src_v, src_s,
    in_sem, idx_sem, send_sem, recv_sem, halo_send, halo_recv, out_sem, ready,
):
    band, z = lax.axis_index("band"), lax.axis_index("patch")
    x, y, core = band // 8, (band // 2) % 4, band % 2

    def loads():
        pairs = (
            (sender_hbm, sender), (feat_hbm, feat), (length_hbm, length), (embed_hbm, embed), (vec_hbm, vec),
            (target_hbm, target), (src_hbm, src), (halo_hbm, halo_ids), (send_hbm, wsend), (agg_hbm, wagg),
            (wsrc_hbm, wsrc), (wdst_hbm, wdst), (wup_hbm, wup), (wdown_hbm, wdown), (gain_hbm, gain),
        )
        return [pltpu.make_async_copy(a, b, in_sem.at[i]) for i, (a, b) in enumerate(pairs)]

    plane = [((((x + i) % 4) * 4 + (y + j) % 4) * 2 + core, z) for i in range(4) for j in range(4) if i or j]
    line = [(band // 2 * 2 + (core + i) % 2, (z + j) % 4) for i in range(2) for j in range(4) if i or j]
    barrier = pltpu.get_barrier_semaphore()
    for device in plane + line:
        pl.semaphore_signal(barrier, inc=1, device_id=device, device_id_type=MESH)

    copies = loads()
    for copy in copies:
        copy.start()

    block = lanes((1, TILE)) // SLOTS

    def sign(piece, way):
        return 1 - 2 * core if way == 1 else 2 * ((core + piece % 2) % 2) - 1

    def band_at(part, piece, way):
        i, j, w = piece // 2, piece % 2, part // 4
        s = sign(piece, way)
        return ((x + 4 + s * i) % 4 * 4 + (y + 8 + s * (i + w)) % 4) * 2 + (core + j) % 2

    def z_at(part, piece, way):
        return (z + 4 + sign(piece, way) * (part % 4)) % 4

    def turn(ref, turned):
        for q in range(4):
            turned[q] = pltpu.roll(ref[...], (4 - z + q) % 4 * SLOTS, 1)

    def pieces(turned, part, half, way):
        row = None
        for p in range(4):
            got = turned[(p + 4 + z - z_at(part, p, way)) % 4, pl.ds(band_at(part, half * 4 + p, way), 1), :]
            row = got if row is None else jnp.where(block == p, got, row)
        return row

    def gather_part(part):
        for half in range(2):
            ids = column(pieces(sender_turned, part, half, 1))
            for k in range(GRID // TILE):
                hit = ids == lanes((TILE, TILE)) + k * TILE
                pick[half * TILE : (half + 1) * TILE, k * TILE : (k + 1) * TILE] = hit.astype(F32).astype(BF16)
        both = lax.dot_general(
            pick[...], feat_pad[...], (((1,), (1,)), ((), ())), preferred_element_type=F32
        )
        for half in range(2):
            rows = both[half * TILE : (half + 1) * TILE, :]
            long = column(pieces(length_turned, part, half, 1))
            first = long.astype(BF16).astype(F32)
            second = (long - first).astype(BF16).astype(F32)
            third = long - first - second
            lane = lanes((TILE, TILE)) + TILE
            tail = rows[:, TILE:]
            tail = jnp.where(lane == VARS, first, tail)
            tail = jnp.where(lane == VARS + 1, second, tail)
            tail = jnp.where(lane == VARS + 2, third, tail)
            to = slice(half * TILE, (half + 1) * TILE)
            outbox[part, to, 0:TILE] = rows[:, :TILE].astype(BF16)
            outbox[part, to, TILE:W] = tail.astype(BF16)

    def send_part(part):
        to_z = z_at(part, 0, 1)
        for piece in range(8):
            rows = outbox.at[part, pl.ds(piece * SLOTS, SLOTS)]
            there = inbox.at[part, pl.ds(piece * SLOTS, SLOTS)]

            def remote():
                pltpu.make_async_remote_copy(
                    src_ref=rows, dst_ref=there, send_sem=send_sem.at[part], recv_sem=recv_sem.at[part],
                    device_id=(band_at(part, piece, 1), to_z), device_id_type=MESH,
                ).start()

            if piece == 0:
                pl.when(part != 0)(remote)

                @pl.when(part == 0)
                def _():
                    pltpu.make_async_copy(rows, there, recv_sem.at[part]).start()
            else:
                remote()

    def wait_sent(part):
        @pl.when(part == 0)
        def _():
            rows = inbox.at[0, pl.ds(0, 7 * SLOTS)]
            pltpu.make_async_copy(rows, rows, send_sem.at[0]).wait()

        @pl.when(part != 0)
        def _():
            pltpu.make_async_copy(inbox.at[part], inbox.at[part], send_sem.at[part]).wait()

    pl.semaphore_wait(barrier, len(plane) + len(line))
    for device in line:
        pl.semaphore_signal(ready, inc=1, device_id=device, device_id_type=MESH)
    feat_pad[W - 32 : W, :] = jnp.zeros((32, GRID), BF16)
    copies[0].wait()
    turn(sender, sender_turned)
    copies[2].wait()
    turn(length, length_turned)
    copies[1].wait()
    feat_pad[0:VARS, :] = feat[...]
    gather_part(0)
    pl.semaphore_wait(ready, len(line))
    send_part(0)

    @pl.loop(1, AHEAD)
    def _(part):
        gather_part(part)
        send_part(part)

    for copy in copies[3:]:
        copy.wait()
    wcat[...] = jnp.zeros((W, 2 * D), BF16)
    wcat[0:VARS, 0:D] = (embed[...].astype(F32) * 0.5).astype(BF16)
    edge_row = jnp.broadcast_to((vec[...].astype(F32) * 0.5)[None, :], (3, D)).astype(BF16)
    wcat[VARS : VARS + 3, D : 2 * D] = edge_row
    parity = (lanes((1, TILE)) + 1) % 2 * 4 + 4
    for k in range(DEG):
        for j in range(M // TILE):
            ids = src[k : k + 1, j * TILE : (j + 1) * TILE] * 4 + parity
            src_v[pl.ds(k * M + j * TILE, TILE)] = ids.reshape(TILE)
    src_copy = pltpu.make_async_copy(src_v, src_s, idx_sem)
    src_copy.start()
    for i in range(4):
        ids = column(halo_ids[i : i + 1, :])
        for k in range(M // TILE):
            hit = ids == lanes((TILE, TILE)) + k * TILE
            halo_pick[i * TILE : (i + 1) * TILE, k * TILE : (k + 1) * TILE] = hit.astype(F32).astype(BF16)
    turn(target, target_turned)
    summed[...] = jnp.zeros((M, D), F32)
    ends = (M + 4 * HALO) * 4 + 8
    table[0:8, :] = jnp.zeros((8, TILE), F32)
    table[ends : ends + 8, :] = jnp.zeros((8, TILE), F32)

    @pl.loop(0, 16 // STEP)
    def _(step):
        for h in range(STEP):
            wait_sent(step * STEP + h)

        @pl.when(step * STEP + AHEAD < 16)
        def _():
            @pl.loop(0, STEP)
            def _(h):
                gather_part(step * STEP + AHEAD + h)
                send_part(step * STEP + AHEAD + h)

        for h in range(STEP * 2):
            ids = jnp.broadcast_to(pieces(target_turned, step * STEP + h // 2, h % 2, -1), (TILE, TILE))
            for k in range(M // TILE):
                hit = ids == lax.broadcasted_iota(jnp.int32, (TILE, TILE), 0) + k * TILE
                scatter[k * TILE : (k + 1) * TILE, h * TILE : (h + 1) * TILE] = hit.astype(F32).astype(BF16)
        for h in range(STEP):
            part = step * STEP + h
            pltpu.make_async_copy(inbox.at[part], inbox.at[part], recv_sem.at[part]).wait()
        rows = inbox[pl.ds(step * STEP, STEP)].reshape(STEP * CHUNK, W)
        latent = half_silu(dot(rows, wcat[:, :D])).astype(BF16)
        pre = dot(latent, wsend[...]) * 0.5 + dot(rows[:, TILE:], wcat[TILE:, D:])
        msgs[...] = half_silu(pre).astype(BF16)
        for k in range(M // CHUNK):
            rows = slice(k * CHUNK, (k + 1) * CHUNK)
            summed[rows, :] += dot(scatter[rows, :], msgs[...])

    neighbours = ((band, (z + 1) % 4), (band, (z + 3) % 4), ((band + 1) % 32, z), ((band + 31) % 32, z))
    low = lax.broadcasted_iota(jnp.int32, (8, TILE), 0) < 4

    def send_halos(layer, values):
        copies = []
        for i in range(4):
            rows = slice(i * HALO, (i + 1) * HALO)
            if i % 2 == 0:
                both = slice(i * HALO, (i + 2) * HALO)
                halo_out[layer, both, :] = dot(halo_pick[both, :], values[...]).astype(BF16)
            copy = pltpu.make_async_remote_copy(
                src_ref=halo_out.at[layer, rows], dst_ref=halo_in.at[layer, rows],
                send_sem=halo_send.at[layer, i], recv_sem=halo_recv.at[layer, i],
                device_id=neighbours[i], device_id_type=MESH,
            )
            copy.start()
            copies.append(copy)
        return copies

    def aggregated(sums_16):
        return half_silu(dot(sums_16, wagg[...]) * 0.5).astype(BF16)

    def updated(layer, own, first, sums_16):
        hidden = half_silu((first + dot(sums_16, wup[layer, D : 2 * D, :])) * 0.5).astype(BF16)
        mixed = dot(hidden, wdown[layer])
        centre = mixed - jnp.mean(mixed, axis=1, keepdims=True)
        spread = jnp.mean(centre * centre, axis=1, keepdims=True)
        normed = centre * lax.rsqrt(spread + 1e-05) * gain[layer : layer + 1, :]
        return (own.astype(F32) + normed).astype(BF16)

    def project(layer):
        for k in range(M // CHUNK):
            rows = slice(k * CHUNK, (k + 1) * CHUNK)
            own = ext[rows, :]
            put_rows(table, 8 + k * CHUNK * 4, dot(own, wsrc[layer]) * 0.5)
            put_rows(recv, k * CHUNK * 4, dot(own, wdst[layer]) * 0.5)
            up[rows, :] = dot(own, wup[layer, 0:D, :])

    def edges():
        @pl.loop(0, M // 2 // PAIRS)
        def _(t):
            for u in range(PAIRS):
                at = pl.ds(pl.multiple_of((t * PAIRS + u) * 8, 8), 8)
                here = recv[at, :]
                total = None
                for k in range(DEG):
                    a = src_s.at[pl.ds(k * M + 2 * u, M - 2 * PAIRS + 1)][t * (2 * PAIRS)]
                    b = src_s.at[pl.ds(k * M + 2 * u + 1, M - 2 * PAIRS + 1)][t * (2 * PAIRS)]
                    h = jnp.where(low, table[pl.ds(a, 8), :], table[pl.ds(b, 8), :]) + here
                    s = half_silu(h)
                    total = s if total is None else total + s
                sums[at, :] = total

        for k in range(M // CHUNK):
            rows = slice(k * CHUNK, (k + 1) * CHUNK)
            for j in range(D // TILE):
                esum[rows, j * TILE : (j + 1) * TILE] = sums[pl.ds(k * CHUNK * 4 + j, CHUNK, stride=4), :].astype(BF16)

    def put_halos(layer, i, rows):
        value = dot(rows, wsrc[layer]) * 0.5
        below, above = value[:HALO], value[HALO:]
        if i == 2:
            below = jnp.where(band == 0, 0.0, below)
            above = jnp.where(band == 31, 0.0, above)
        put_rows(table, 8 + (M + i * HALO) * 4, below)
        put_rows(table, 8 + (M + (i + 1) * HALO) * 4, above)

    esum[...] = summed[...].astype(BF16)
    halos = send_halos(0, esum)
    for k in range(M // CHUNK):
        rows = slice(k * CHUNK, (k + 1) * CHUNK)
        ext[rows, :] = aggregated(esum[rows, :])
    project(0)
    src_copy.wait()
    for i in (2, 0):
        rows = slice(i * HALO, (i + 2) * HALO)
        halos[i].wait()
        halos[i + 1].wait()
        halo_now[rows, :] = aggregated(halo_in[0, rows, :])
        put_halos(0, i, halo_now[rows, :])
    edges()

    halos = send_halos(1, esum)
    for k in range(M // CHUNK):
        rows = slice(k * CHUNK, (k + 1) * CHUNK)
        ext[rows, :] = updated(0, ext[rows, :], up[rows, :], esum[rows, :])
    for k in range(2):
        rows = slice(k * CHUNK, (k + 1) * CHUNK)
        halo_up[rows, :] = dot(halo_now[rows, :], wup[0, 0:D, :])
    project(1)
    for i in (2, 0):
        rows = slice(i * HALO, (i + 2) * HALO)
        halos[i].wait()
        halos[i + 1].wait()
        put_halos(1, i, updated(0, halo_now[rows, :], halo_up[rows, :], halo_in[1, rows, :]))
    edges()
    for k in range(M // CHUNK):
        rows = slice(k * CHUNK, (k + 1) * CHUNK)
        ext[rows, :] = updated(1, ext[rows, :], up[rows, :], esum[rows, :])
        pltpu.make_async_copy(ext.at[rows], out_hbm.at[rows], out_sem).start()
    pltpu.make_async_copy(ext, out_hbm, out_sem).wait()


def on_device(
    grid_feat, w_embed, w_send, edge_vec, g2m_sender, g2m_weight, g2m_target, w_agg, halo_rows, mesh_src,
    w_src, w_dst, w_up, w_down, ln_gain,
):
    args = (
        grid_feat.T, w_embed, w_send, edge_vec, g2m_sender.reshape(32, TILE), g2m_weight.reshape(32, TILE),
        g2m_target.reshape(32, TILE), w_agg, halo_rows.reshape(4, HALO), mesh_src.T, w_src, w_dst, w_up, w_down, ln_gain,
    )
    VM = pltpu.VMEM
    staged = [VM(a.shape, a.dtype) for a in args]
    scratch = [
        VM((W, GRID), BF16),
        VM((W, 2 * D), BF16),
        VM((CHUNK, GRID), BF16),
        VM((16, CHUNK, W), BF16),
        VM((16, CHUNK, W), BF16),
        VM((4, 32, TILE), jnp.int32),
        VM((4, 32, TILE), F32),
        VM((4, 32, TILE), jnp.int32),
        VM((M, STEP * CHUNK), BF16),
        VM((STEP * CHUNK, D), BF16),
        VM((M, D), F32),
        VM((M, D), BF16),
        VM((4 * HALO, M), BF16),
        VM((LAYERS, 4 * HALO, D), BF16),
        VM((LAYERS, 4 * HALO, D), BF16),
        VM((4 * HALO, D), BF16),
        VM((4 * HALO, D), F32),
        VM(((M + 4 * HALO) * 4 + 16, TILE), F32),
        VM((M * 4, TILE), F32),
        VM((M * 4, TILE), F32),
        VM((M, D), BF16),
        VM((M, D), F32),
        VM((DEG * M,), jnp.int32),
        pltpu.SMEM((DEG * M,), jnp.int32),
        pltpu.SemaphoreType.DMA((len(args),)),
        pltpu.SemaphoreType.DMA,
        pltpu.SemaphoreType.DMA((16,)),
        pltpu.SemaphoreType.DMA((16,)),
        pltpu.SemaphoreType.DMA((LAYERS, 4)),
        pltpu.SemaphoreType.DMA((LAYERS, 4)),
        pltpu.SemaphoreType.DMA,
        pltpu.SemaphoreType.REGULAR,
    ]
    anywhere = pl.BlockSpec(memory_space=pl.ANY)
    return pl.pallas_call(
        kernel,
        out_shape=jax.ShapeDtypeStruct((M, D), BF16),
        in_specs=[anywhere] * len(args),
        out_specs=anywhere,
        scratch_shapes=staged + scratch,
        compiler_params=pltpu.CompilerParams(collective_id=0, has_side_effects=True, vmem_limit_bytes=56 * 2**20),
    )(*args)


def solution(mesh):
    split = P(("band", "patch"), None)
    return jax.shard_map(
        on_device,
        mesh=mesh,
        in_specs=(
            split, P(), P(), P(), split, split, split, P(), P(("band", "patch"), None, None), split,
            P(), P(), P(), P(), P(),
        ),
        out_specs=split,
        check_vma=False,
    )
```

```python
import jax
import jax.numpy as jnp
from jax import lax
from jax.experimental import pallas as pl
from jax.experimental.pallas import tpu as pltpu
from jax.sharding import PartitionSpec as P

MESH = pl.DeviceIdType.MESH
BF16 = jnp.bfloat16
F32 = jnp.float32
VARS, D, W = 227, 512, 256
GRID, M, SLOTS = 2048, 1024, 32
HALO, DEG, LAYERS = 128, 6, 2
TILE = 128
CHUNK = 256
BIG = 512
PAIRS = 16
AHEAD = 6
STEP = 2


def dot(a, b):
    return jnp.dot(a, b, preferred_element_type=F32)


def half_silu(h):
    return h + h * jnp.tanh(h)


def column(row):
    return jnp.transpose(jnp.broadcast_to(row, (TILE, TILE)))


def lanes(shape):
    return lax.broadcasted_iota(jnp.int32, shape, len(shape) - 1)


def put_rows(ref, at, value):
    rows = value.shape[0]
    for j in range(D // TILE):
        ref[pl.ds(at + j, rows, stride=4), :] = value[:, j * TILE : (j + 1) * TILE]


def kernel(
    feat_hbm, embed_hbm, send_hbm, vec_hbm, sender_hbm, length_hbm, target_hbm, agg_hbm, halo_hbm, src_hbm,
    wsrc_hbm, wdst_hbm, wup_hbm, wdown_hbm, gain_hbm,
    out_hbm,
    feat, embed, wsend, vec, sender, length, target, wagg, halo_ids, src, wsrc, wdst, wup, wdown, gain,
    feat_pad, wcat, pick, outbox, inbox, sender_turned, length_turned, target_turned, scatter, msgs, summed, ext, halo_pick, halo_out, halo_in,
    halo_now, halo_up, table, recv, sums, esum, up, src_v, src_s,
    in_sem, idx_sem, send_sem, recv_sem, halo_send, halo_recv, out_sem, ready,
):
    band, z = lax.axis_index("band"), lax.axis_index("patch")
    x, y, core = band // 8, (band // 2) % 4, band % 2

    def loads():
        pairs = (
            (sender_hbm, sender), (feat_hbm, feat), (length_hbm, length), (embed_hbm, embed), (vec_hbm, vec),
            (target_hbm, target), (src_hbm, src), (halo_hbm, halo_ids), (send_hbm, wsend), (agg_hbm, wagg),
            (wsrc_hbm, wsrc), (wdst_hbm, wdst), (wup_hbm, wup), (wdown_hbm, wdown), (gain_hbm, gain),
        )
        return [pltpu.make_async_copy(a, b, in_sem.at[i]) for i, (a, b) in enumerate(pairs)]

    plane = [((((x + i) % 4) * 4 + (y + j) % 4) * 2 + core, z) for i in range(4) for j in range(4) if i or j]
    line = [(band // 2 * 2 + (core + i) % 2, (z + j) % 4) for i in range(2) for j in range(4) if i or j]
    barrier = pltpu.get_barrier_semaphore()
    for device in plane + line:
        pl.semaphore_signal(barrier, inc=1, device_id=device, device_id_type=MESH)

    copies = loads()
    for copy in copies:
        copy.start()

    block = lanes((1, TILE)) // SLOTS

    def sign(piece, way):
        return 1 - 2 * core if way == 1 else 2 * ((core + piece % 2) % 2) - 1

    def band_at(part, piece, way):
        i, j, w = piece // 2, piece % 2, part // 4
        s = sign(piece, way)
        return ((x + 4 + s * i) % 4 * 4 + (y + 8 + s * (i + w)) % 4) * 2 + (core + j) % 2

    def z_at(part, piece, way):
        return (z + 4 + sign(piece, way) * (part % 4)) % 4

    def turn(ref, turned):
        for q in range(4):
            turned[q] = pltpu.roll(ref[...], (4 - z + q) % 4 * SLOTS, 1)

    def pieces(turned, part, half, way):
        row = None
        for p in range(4):
            got = turned[(p + 4 + z - z_at(part, p, way)) % 4, pl.ds(band_at(part, half * 4 + p, way), 1), :]
            row = got if row is None else jnp.where(block == p, got, row)
        return row

    def gather_part(part):
        for half in range(2):
            ids = column(pieces(sender_turned, part, half, 1))
            for k in range(GRID // TILE):
                hit = ids == lanes((TILE, TILE)) + k * TILE
                pick[half * TILE : (half + 1) * TILE, k * TILE : (k + 1) * TILE] = hit.astype(F32).astype(BF16)
        both = lax.dot_general(
            pick[...], feat_pad[...], (((1,), (1,)), ((), ())), preferred_element_type=F32
        )
        for half in range(2):
            rows = both[half * TILE : (half + 1) * TILE, :]
            long = column(pieces(length_turned, part, half, 1))
            first = long.astype(BF16).astype(F32)
            second = (long - first).astype(BF16).astype(F32)
            third = long - first - second
            lane = lanes((TILE, TILE)) + TILE
            tail = rows[:, TILE:]
            tail = jnp.where(lane == VARS, first, tail)
            tail = jnp.where(lane == VARS + 1, second, tail)
            tail = jnp.where(lane == VARS + 2, third, tail)
            to = slice(half * TILE, (half + 1) * TILE)
            outbox[part, to, 0:TILE] = rows[:, :TILE].astype(BF16)
            outbox[part, to, TILE:W] = tail.astype(BF16)

    def send_part(part):
        to_z = z_at(part, 0, 1)
        for piece in range(8):
            rows = outbox.at[part, pl.ds(piece * SLOTS, SLOTS)]
            there = inbox.at[part, pl.ds(piece * SLOTS, SLOTS)]

            def remote():
                pltpu.make_async_remote_copy(
                    src_ref=rows, dst_ref=there, send_sem=send_sem.at[part], recv_sem=recv_sem.at[part],
                    device_id=(band_at(part, piece, 1), to_z), device_id_type=MESH,
                ).start()

            if piece == 0:
                pl.when(part != 0)(remote)

                @pl.when(part == 0)
                def _():
                    pltpu.make_async_copy(rows, there, recv_sem.at[part]).start()
            else:
                remote()

    def wait_sent(part):
        @pl.when(part == 0)
        def _():
            rows = inbox.at[0, pl.ds(0, 7 * SLOTS)]
            pltpu.make_async_copy(rows, rows, send_sem.at[0]).wait()

        @pl.when(part != 0)
        def _():
            pltpu.make_async_copy(inbox.at[part], inbox.at[part], send_sem.at[part]).wait()

    pl.semaphore_wait(barrier, len(plane) + len(line))
    for device in line:
        pl.semaphore_signal(ready, inc=1, device_id=device, device_id_type=MESH)
    feat_pad[W - 32 : W, :] = jnp.zeros((32, GRID), BF16)
    copies[0].wait()
    turn(sender, sender_turned)
    copies[2].wait()
    turn(length, length_turned)
    copies[1].wait()
    feat_pad[0:VARS, :] = feat[...]
    gather_part(0)
    pl.semaphore_wait(ready, len(line))
    send_part(0)

    @pl.loop(1, AHEAD)
    def _(part):
        gather_part(part)
        send_part(part)

    for copy in copies[3:]:
        copy.wait()
    wcat[...] = jnp.zeros((W, 2 * D), BF16)
    wcat[0:VARS, 0:D] = (embed[...].astype(F32) * 0.5).astype(BF16)
    edge_row = jnp.broadcast_to((vec[...].astype(F32) * 0.5)[None, :], (3, D)).astype(BF16)
    wcat[VARS : VARS + 3, D : 2 * D] = edge_row
    parity = (lanes((1, TILE)) + 1) % 2 * 4 + 4
    for k in range(DEG):
        for j in range(M // TILE):
            ids = src[k : k + 1, j * TILE : (j + 1) * TILE] * 4 + parity
            src_v[pl.ds(k * M + j * TILE, TILE)] = ids.reshape(TILE)
    src_copy = pltpu.make_async_copy(src_v, src_s, idx_sem)
    src_copy.start()
    for i in range(4):
        ids = column(halo_ids[i : i + 1, :])
        for k in range(M // TILE):
            hit = ids == lanes((TILE, TILE)) + k * TILE
            halo_pick[i * TILE : (i + 1) * TILE, k * TILE : (k + 1) * TILE] = hit.astype(F32).astype(BF16)
    turn(target, target_turned)
    summed[...] = jnp.zeros((M, D), F32)
    ends = (M + 4 * HALO) * 4 + 8
    table[0:8, :] = jnp.zeros((8, TILE), F32)
    table[ends : ends + 8, :] = jnp.zeros((8, TILE), F32)

    @pl.loop(0, 16 // STEP)
    def _(step):
        for h in range(STEP):
            wait_sent(step * STEP + h)

        @pl.when(step * STEP + AHEAD < 16)
        def _():
            @pl.loop(0, STEP)
            def _(h):
                gather_part(step * STEP + AHEAD + h)
                send_part(step * STEP + AHEAD + h)

        for h in range(STEP * 2):
            ids = jnp.broadcast_to(pieces(target_turned, step * STEP + h // 2, h % 2, -1), (TILE, TILE))
            for k in range(M // TILE):
                hit = ids == lax.broadcasted_iota(jnp.int32, (TILE, TILE), 0) + k * TILE
                scatter[k * TILE : (k + 1) * TILE, h * TILE : (h + 1) * TILE] = hit.astype(F32).astype(BF16)
        for h in range(STEP):
            part = step * STEP + h
            pltpu.make_async_copy(inbox.at[part], inbox.at[part], recv_sem.at[part]).wait()
        rows = inbox[pl.ds(step * STEP, STEP)].reshape(STEP * CHUNK, W)
        latent = half_silu(dot(rows, wcat[:, :D])).astype(BF16)
        pre = dot(latent, wsend[...]) * 0.5 + dot(rows[:, TILE:], wcat[TILE:, D:])
        msgs[...] = half_silu(pre).astype(BF16)
        for k in range(M // BIG):
            rows = slice(k * BIG, (k + 1) * BIG)
            summed[rows, :] += dot(scatter[rows, :], msgs[...])

    neighbours = ((band, (z + 1) % 4), (band, (z + 3) % 4), ((band + 1) % 32, z), ((band + 31) % 32, z))
    low = lax.broadcasted_iota(jnp.int32, (8, TILE), 0) < 4

    def send_halos(layer, values):
        copies = []
        for i in range(4):
            rows = slice(i * HALO, (i + 1) * HALO)
            if i % 2 == 0:
                both = slice(i * HALO, (i + 2) * HALO)
                halo_out[layer, both, :] = dot(halo_pick[both, :], values[...]).astype(BF16)
            copy = pltpu.make_async_remote_copy(
                src_ref=halo_out.at[layer, rows], dst_ref=halo_in.at[layer, rows],
                send_sem=halo_send.at[layer, i], recv_sem=halo_recv.at[layer, i],
                device_id=neighbours[i], device_id_type=MESH,
            )
            copy.start()
            copies.append(copy)
        return copies

    def aggregated(sums_16):
        return half_silu(dot(sums_16, wagg[...]) * 0.5).astype(BF16)

    def updated(layer, own, first, sums_16):
        hidden = half_silu((first + dot(sums_16, wup[layer, D : 2 * D, :])) * 0.5).astype(BF16)
        mixed = dot(hidden, wdown[layer])
        centre = mixed - jnp.mean(mixed, axis=1, keepdims=True)
        spread = jnp.mean(centre * centre, axis=1, keepdims=True)
        normed = centre * lax.rsqrt(spread + 1e-05) * gain[layer : layer + 1, :]
        return (own.astype(F32) + normed).astype(BF16)

    def project(layer):
        for k in range(M // BIG):
            rows = slice(k * BIG, (k + 1) * BIG)
            own = ext[rows, :]
            put_rows(table, 8 + k * BIG * 4, dot(own, wsrc[layer]) * 0.5)
            put_rows(recv, k * BIG * 4, dot(own, wdst[layer]) * 0.5)
            up[rows, :] = dot(own, wup[layer, 0:D, :])

    def edges():
        @pl.loop(0, M // 2 // PAIRS)
        def _(t):
            for u in range(PAIRS):
                at = pl.ds(pl.multiple_of((t * PAIRS + u) * 8, 8), 8)
                here = recv[at, :]
                total = None
                for k in range(DEG):
                    a = src_s.at[pl.ds(k * M + 2 * u, M - 2 * PAIRS + 1)][t * (2 * PAIRS)]
                    b = src_s.at[pl.ds(k * M + 2 * u + 1, M - 2 * PAIRS + 1)][t * (2 * PAIRS)]
                    h = jnp.where(low, table[pl.ds(a, 8), :], table[pl.ds(b, 8), :]) + here
                    s = half_silu(h)
                    total = s if total is None else total + s
                sums[at, :] = total

        for k in range(M // CHUNK):
            rows = slice(k * CHUNK, (k + 1) * CHUNK)
            for j in range(D // TILE):
                esum[rows, j * TILE : (j + 1) * TILE] = sums[pl.ds(k * CHUNK * 4 + j, CHUNK, stride=4), :].astype(BF16)

    def put_halos(layer, i, rows):
        value = dot(rows, wsrc[layer]) * 0.5
        below, above = value[:HALO], value[HALO:]
        if i == 2:
            below = jnp.where(band == 0, 0.0, below)
            above = jnp.where(band == 31, 0.0, above)
        put_rows(table, 8 + (M + i * HALO) * 4, below)
        put_rows(table, 8 + (M + (i + 1) * HALO) * 4, above)

    esum[...] = summed[...].astype(BF16)
    halos = send_halos(0, esum)
    for k in range(M // CHUNK):
        rows = slice(k * CHUNK, (k + 1) * CHUNK)
        ext[rows, :] = aggregated(esum[rows, :])
    project(0)
    src_copy.wait()
    for i in (2, 0):
        rows = slice(i * HALO, (i + 2) * HALO)
        halos[i].wait()
        halos[i + 1].wait()
        halo_now[rows, :] = aggregated(halo_in[0, rows, :])
        put_halos(0, i, halo_now[rows, :])
    edges()

    halos = send_halos(1, esum)
    for k in range(M // CHUNK):
        rows = slice(k * CHUNK, (k + 1) * CHUNK)
        ext[rows, :] = updated(0, ext[rows, :], up[rows, :], esum[rows, :])
    for k in range(2):
        rows = slice(k * CHUNK, (k + 1) * CHUNK)
        halo_up[rows, :] = dot(halo_now[rows, :], wup[0, 0:D, :])
    project(1)
    for i in (2, 0):
        rows = slice(i * HALO, (i + 2) * HALO)
        halos[i].wait()
        halos[i + 1].wait()
        put_halos(1, i, updated(0, halo_now[rows, :], halo_up[rows, :], halo_in[1, rows, :]))
    edges()
    for k in range(M // CHUNK):
        rows = slice(k * CHUNK, (k + 1) * CHUNK)
        ext[rows, :] = updated(1, ext[rows, :], up[rows, :], esum[rows, :])
        pltpu.make_async_copy(ext.at[rows], out_hbm.at[rows], out_sem).start()
    pltpu.make_async_copy(ext, out_hbm, out_sem).wait()


def on_device(
    grid_feat, w_embed, w_send, edge_vec, g2m_sender, g2m_weight, g2m_target, w_agg, halo_rows, mesh_src,
    w_src, w_dst, w_up, w_down, ln_gain,
):
    args = (
        grid_feat.T, w_embed, w_send, edge_vec, g2m_sender.reshape(32, TILE), g2m_weight.reshape(32, TILE),
        g2m_target.reshape(32, TILE), w_agg, halo_rows.reshape(4, HALO), mesh_src.T, w_src, w_dst, w_up, w_down, ln_gain,
    )
    VM = pltpu.VMEM
    staged = [VM(a.shape, a.dtype) for a in args]
    scratch = [
        VM((W, GRID), BF16),
        VM((W, 2 * D), BF16),
        VM((CHUNK, GRID), BF16),
        VM((16, CHUNK, W), BF16),
        VM((16, CHUNK, W), BF16),
        VM((4, 32, TILE), jnp.int32),
        VM((4, 32, TILE), F32),
        VM((4, 32, TILE), jnp.int32),
        VM((M, STEP * CHUNK), BF16),
        VM((STEP * CHUNK, D), BF16),
        VM((M, D), F32),
        VM((M, D), BF16),
        VM((4 * HALO, M), BF16),
        VM((LAYERS, 4 * HALO, D), BF16),
        VM((LAYERS, 4 * HALO, D), BF16),
        VM((4 * HALO, D), BF16),
        VM((4 * HALO, D), F32),
        VM(((M + 4 * HALO) * 4 + 16, TILE), F32),
        VM((M * 4, TILE), F32),
        VM((M * 4, TILE), F32),
        VM((M, D), BF16),
        VM((M, D), F32),
        VM((DEG * M,), jnp.int32),
        pltpu.SMEM((DEG * M,), jnp.int32),
        pltpu.SemaphoreType.DMA((len(args),)),
        pltpu.SemaphoreType.DMA,
        pltpu.SemaphoreType.DMA((16,)),
        pltpu.SemaphoreType.DMA((16,)),
        pltpu.SemaphoreType.DMA((LAYERS, 4)),
        pltpu.SemaphoreType.DMA((LAYERS, 4)),
        pltpu.SemaphoreType.DMA,
        pltpu.SemaphoreType.REGULAR,
    ]
    anywhere = pl.BlockSpec(memory_space=pl.ANY)
    return pl.pallas_call(
        kernel,
        out_shape=jax.ShapeDtypeStruct((M, D), BF16),
        in_specs=[anywhere] * len(args),
        out_specs=anywhere,
        scratch_shapes=staged + scratch,
        compiler_params=pltpu.CompilerParams(collective_id=0, has_side_effects=True, vmem_limit_bytes=56 * 2**20),
    )(*args)


def solution(mesh):
    split = P(("band", "patch"), None)
    return jax.shard_map(
        on_device,
        mesh=mesh,
        in_specs=(
            split, P(), P(), P(), split, split, split, P(), P(("band", "patch"), None, None), split,
            P(), P(), P(), P(), P(),
        ),
        out_specs=split,
        check_vma=False,
    )
```
